32 devices in a mesh: tm: 4 (over x, core), dom: 8 (over z, y).
Axes of the slice: x: 2, y: 2, z: 4, core: 2. Of those that a mesh axis runs over, the one named last changes fastest.
Arguments:
- features: bfloat16 [8, 4096, 128], P('tm', 'dom'), may hold values from -6 to 6
- tile_values: bfloat16 [8, 32, 8, 4, 128, 128], P('tm', 'dom'), may hold values from -0.125 to 0.125
- tile_cols: int32 [8, 32, 8, 4], P('tm', 'dom'), may hold values from 0 to 3
- tile_count: int32 [8, 32, 8], P('tm', 'dom'), may hold values from 0 to 4, as said below
- hidden_start: float32 [4096, 512], P('dom'), may hold values from -4 to 4
- w_graph: bfloat16 [128, 512], replicated, may hold values from -0.5 to 0.5
- w_input: bfloat16 [512, 1536], replicated, may hold values from -0.25 to 0.25
- w_hidden: bfloat16 [512, 1536], replicated, may hold values from -0.25 to 0.25
- update_bias: float32 [512], replicated, may hold values from -1 to 4
Outputs:
- hidden_seq: bfloat16 [8, 4096, 512], P('tm', 'dom')
The draws below stay inside these ranges and needn't reach their ends.
Inputs may be any that keep to these rules, and one draw needn't show every extreme that they name: `tile_count`: number of live slots; for each row block the entry of its own partition is 4.
All inputs are finite; a program needn't handle non-finite values.
Results may differ from the reference program's by a relative error of at most 0.0052.
Values may be sent and summed in bfloat16 or wider, within the bound.
No kernel may reach another device: no remote copies, remote signals or barrier semaphores. Data moves between devices by JAX's collectives and lax.ppermute only.
A program may use at most 128 MiB of HBM per device.

```python
import jax
import jax.numpy as jnp
from jax import lax

H = 512
F = 128
BLK = 128
KP = 4
SNAPS = 8
NODES = 4096
NB_DEV = 4
NBLK = 32
N_DOM = 8


def draw_tile_count(key, part):
    base = jax.random.randint(key, (SNAPS, NBLK, N_DOM), 0, KP + 1)
    owner = (jnp.arange(NBLK, dtype=jnp.int32) // NB_DEV)[None, :, None]
    source = jnp.arange(N_DOM, dtype=jnp.int32)[None, None, :]
    return jnp.where(owner == source, KP, base).astype(jnp.int32)


def with_ends(array, key, smallest, top_value):
    longest = array.shape.index(max(array.shape))
    spots = []
    for shift in (0, 1):
        where = [jax.random.randint(jax.random.fold_in(key, axis), (), 0, length) for axis, length in enumerate(array.shape)]
        where[longest] = (where[longest] + shift) % array.shape[longest]
        spots.append(tuple(where))
    return array.at[spots[0]].set(smallest).at[spots[1]].set(top_value)


def levels(key, dims, cuts, smallest, high):
    def one(position, shards_of):
        heights = jax.random.uniform(jax.random.fold_in(jax.random.fold_in(key, 6), position), (shards_of,), jnp.float32, smallest / len(cuts), high / len(cuts))
        return jnp.repeat(jnp.exp(heights), dims[position] // shards_of).reshape((-1,) + (1,) * (len(dims) - position - 1))

    gain = one(*cuts[0])
    for cut in cuts[1:]:
        gain = gain * one(*cut)
    return gain


def scatter_about(own_key, extent, scale, most, cuts=(), kind=jnp.bfloat16):
    entries = jax.random.normal(own_key, extent, jnp.float32) * scale
    if len(cuts) > 0:
        entries = levels(own_key, extent, cuts, -0.22, 0.18) * entries
    return jnp.clip(entries, min=-most, max=most).astype(kind)


def setup_inputs(seed: int = 0) -> dict:
    seeds = jax.random.split(jax.random.key(seed), 10)
    return {
        "features": scatter_about(seeds[0], (SNAPS, NODES, F), 1.0, 6.0, ((0, 4), (1, 8))),
        "tile_values": scatter_about(seeds[1], (SNAPS, NBLK, N_DOM, KP, BLK, BLK), (BLK * KP * N_DOM // 2) ** -0.5, 0.125, ((0, 4), (1, 8))),
        "tile_cols": with_ends(jax.random.randint(seeds[2], (SNAPS, NBLK, N_DOM, KP), 0, NB_DEV), jax.random.fold_in(seeds[2], 1), 0, NB_DEV - 1).astype(jnp.int32),
        "tile_count": draw_tile_count(jax.random.fold_in(seeds[9], 71), 0),
        "hidden_start": scatter_about(seeds[4], (NODES, H), 0.7, 4.0, ((0, 8),), jnp.float32),
        "w_graph": scatter_about(seeds[5], (F, H), F ** -0.5, 0.5),
        "w_input": scatter_about(seeds[6], (H, 3 * H), H ** -0.5, 0.25),
        "w_hidden": scatter_about(seeds[7], (H, 3 * H), H ** -0.5, 0.25),
        "update_bias": jnp.clip(jax.random.uniform(seeds[8], (H,), jnp.float32, -1.0, 4.0), -1.0, 4.0),
    }


def propagate_one(projected, tiles, cols, counts):
    blocks = projected.reshape(NBLK, BLK, H)
    offsets = (jnp.arange(N_DOM, dtype=jnp.int32) * NB_DEV)[:, None]
    slots = jnp.arange(KP, dtype=jnp.int32)[None, :]

    def row_block(args):
        tile_row, col_row, count_row = args
        picked = blocks[(col_row + offsets).astype(jnp.int32)].astype(jnp.float32)
        live = (slots < count_row[:, None]).astype(jnp.float32)
        weighted = tile_row.astype(jnp.float32) * live[:, :, None, None]
        return jnp.einsum("pkij,pkjh->ih", weighted, picked)

    out = lax.map(row_block, (tiles, cols, counts))
    return out.reshape(NODES, H)


def reference(features, tile_values, tile_cols, tile_count, hidden_start, w_graph, w_input, w_hidden, update_bias):
    def graph_step(args):
        feats, tiles, cols, counts = args
        projected = jnp.dot(feats, w_graph, preferred_element_type=jnp.float32).astype(jnp.bfloat16)
        propagated = propagate_one(projected, tiles, cols, counts)
        return jax.nn.relu(propagated).astype(jnp.bfloat16)

    graph_out = lax.map(graph_step, (features, tile_values, tile_cols, tile_count))

    def cell(state, graph_row):
        gx = jnp.dot(graph_row, w_input, preferred_element_type=jnp.float32)
        gh = jnp.dot(state.astype(jnp.bfloat16), w_hidden, preferred_element_type=jnp.float32)
        reset = jax.nn.sigmoid(gx[:, :H] + gh[:, :H])
        update = jax.nn.sigmoid(gx[:, H:2 * H] + gh[:, H:2 * H] + update_bias)
        cand = jnp.tanh(gx[:, 2 * H:] + reset * gh[:, 2 * H:])
        state = update * state + (1.0 - update) * cand
        return state, state.astype(jnp.bfloat16)

    final_state, hidden_seq = lax.scan(cell, hidden_start.astype(jnp.float32), graph_out)
    return hidden_seq
```

```python
import functools

import jax
import jax.numpy as jnp
from jax import lax
from jax.experimental import pallas as pl
from jax.experimental.pallas import tpu as pltpu
from jax.sharding import PartitionSpec as P

BF16 = jnp.bfloat16
F32 = jnp.float32
CORES = 2
CHUNKS = 2
VMEM = pltpu.MemorySpace.VMEM
SMEM = pltpu.MemorySpace.SMEM


def ring_order(size):
    width = 1
    while width * width * 4 <= size:
        width *= 2
    depth = size // width
    walk = [(z, 0) for z in range(depth)]
    for step, z in enumerate(reversed(range(depth))):
        row = range(1, width) if step % 2 == 0 else reversed(range(1, width))
        walk += [(z, y) for y in row]
    return [z * width + y for z, y in walk]


def sigmoid(x):
    return 0.5 * jnp.tanh(0.5 * x) + 0.5


def params():
    return pltpu.CompilerParams(vmem_limit_bytes=24 * 2**20)


def cost(flops, bytes_accessed):
    return pl.CostEstimate(flops=int(flops), bytes_accessed=int(bytes_accessed), transcendentals=0)


def add_partition(tiles, cols, counts, x_ref, snap, row, part, lhs, rhs):
    parts, slots = tiles.shape[2:4]
    blk = tiles.shape[-1]
    rows = tiles.shape[1]
    base = (snap * rows + row) * parts + part
    for k in range(slots):
        col = cols[base * slots + k]
        block = x_ref[pl.ds(pl.multiple_of(col * blk, blk), blk), :]
        rhs.append(jnp.where(k < counts[base], block, jnp.zeros_like(block)))
        lhs.append(tiles[snap, row, part, k])


def spmm_kernel(info, cols, counts, tiles, *refs, pieces, first, last):
    x_refs = refs[: len(pieces)]
    acc_in = None if first else refs[len(pieces)]
    outs = refs[len(pieces) + (0 if first else 1) :]
    snaps, rows = tiles.shape[:2]
    half = rows // CORES
    core = info[0]
    for snap in range(snaps):
        for rel in range(rows):
            row = lax.rem(rel + core * half, rows)
            lhs, rhs = [], []
            for x_ref, (piece_snap, where) in zip(x_refs, pieces):
                if piece_snap == snap:
                    add_partition(tiles, cols, counts, x_ref, snap, row, info[where], lhs, rhs)
            total = jnp.dot(
                jnp.concatenate(lhs, axis=1), jnp.concatenate(rhs, axis=0), preferred_element_type=F32
            )
            if not first:
                total = total + acc_in[snap, rel]
            if last:
                keep, send = outs
                blk = total.shape[0]
                target = keep if rel < half else send
                at = (rel % half) * blk
                target[snap, at : at + blk, :] = total.astype(BF16)
            else:
                outs[0][snap, rel] = total


def spmm(info, cols, counts, tiles, xs, pieces, acc, last):
    snaps, rows, parts, slots, blk, _ = tiles.shape
    feats = xs[0].shape[-1]
    first = acc is None
    operands = [info, cols, counts, tiles, *xs] + ([] if first else [acc])
    specs = [pl.BlockSpec(memory_space=SMEM)] * 3 + [pl.BlockSpec(memory_space=VMEM)] * (len(operands) - 3)
    if last:
        out = jax.ShapeDtypeStruct((snaps, rows // CORES * blk, feats), BF16)
        out_shape = (out, out)
        aliases = {}
    else:
        out_shape = jax.ShapeDtypeStruct((snaps, rows, blk, feats), F32)
        aliases = {} if first else {len(operands) - 1: 0}
    flops = 2 * len(xs) * rows * slots * blk * blk * feats
    return pl.pallas_call(
        functools.partial(spmm_kernel, pieces=pieces, first=first, last=last),
        out_shape=out_shape,
        in_specs=specs,
        out_specs=jax.tree.map(lambda _: pl.BlockSpec(memory_space=VMEM), out_shape),
        input_output_aliases=aliases,
        compiler_params=params(),
        cost_estimate=cost(flops * 4, 2**20),
        name="spmm",
    )(*operands)


def gates(ax, w_graph, w_input):
    snaps, rows, feats = ax.shape
    hid, width = w_input.shape

    def kernel(ax, w_graph, w_input, out):
        graph = jnp.dot(ax[...].reshape(snaps * rows, feats), w_graph[...], preferred_element_type=F32)
        graph = jnp.maximum(graph, 0.0).astype(BF16)
        for j in range(0, width, hid):
            part = jnp.dot(graph, w_input[:, j : j + hid], preferred_element_type=F32)
            out[:, :, j : j + hid] = part.reshape(snaps, rows, hid)

    return pl.pallas_call(
        kernel,
        out_shape=jax.ShapeDtypeStruct((snaps, rows, width), F32),
        in_specs=[pl.BlockSpec(memory_space=VMEM)] * 3,
        out_specs=pl.BlockSpec(memory_space=VMEM),
        compiler_params=params(),
        cost_estimate=cost(2 * snaps * rows * hid * width * 2, 2**20),
        name="gates",
    )(ax, w_graph, w_input)


def recurrence_kernel(info, state_in, gx_own, gx_other, w_hidden, bias, *refs, phase, chunk):
    state_out, keep, send = refs[-3:]
    core, place = info[0], info[1]
    snaps, rows, hid = keep.shape
    at = slice(chunk * rows, (chunk + 1) * rows)
    block = min(256, hid)

    def run(own_first):
        state = state_in[...].astype(F32)
        for step in range(CORES * snaps):
            own = (step < snaps) == own_first
            gx, out, s = (gx_own if own else gx_other), (keep if own else send), step % snaps
            low = state.astype(BF16)
            parts = []
            for j in range(0, hid, block):
                def gate(g):
                    return jnp.dot(low, w_hidden[:, g * hid + j : g * hid + j + block], preferred_element_type=F32)

                def given(g):
                    return gx[s, at, g * hid + j : g * hid + j + block]

                gh_r, gh_c, gh_u = gate(0), gate(2), gate(1)
                reset = sigmoid(given(0) + gh_r)
                cand = jnp.tanh(given(2) + reset * gh_c)
                update = sigmoid(given(1) + gh_u + bias[:, j : j + block])
                parts.append(update * state[:, j : j + block] + (1.0 - update) * cand)
            state = jnp.concatenate(parts, axis=1)
            out[s] = state.astype(BF16)
        state_out[...] = state.astype(BF16)

    @pl.when((place == phase) & (core == 0))
    def _():
        run(True)

    @pl.when((place == phase) & (core != 0))
    def _():
        run(False)


def recurrence(info, state, gx_own, gx_other, w_hidden, bias, hidden, phase, chunk):
    hid = w_hidden.shape[0]
    snaps = gx_own.shape[0]
    rows = gx_own.shape[1] // CHUNKS
    operands = [info, state, gx_own, gx_other, w_hidden, bias] + list(hidden)
    part = jax.ShapeDtypeStruct((snaps, rows, hid), BF16)
    specs = [pl.BlockSpec(memory_space=SMEM)] + [pl.BlockSpec(memory_space=VMEM)] * (len(operands) - 1)
    return pl.pallas_call(
        functools.partial(recurrence_kernel, phase=phase, chunk=chunk),
        out_shape=(jax.ShapeDtypeStruct((rows, hid), BF16), part, part),
        in_specs=specs,
        out_specs=(pl.BlockSpec(memory_space=VMEM),) * 3,
        input_output_aliases={6: 1, 7: 2} if hidden else {},
        compiler_params=params(),
        cost_estimate=cost(2 * CORES * snaps * rows * hid * 3 * hid * 4, 2**20),
        name="recurrence",
    )(*operands)


def per_device(
    features, tile_values, tile_cols, tile_count, hidden_start, w_graph, w_input, w_hidden, update_bias
):
    snaps, nodes, feats = features.shape
    parts = lax.axis_size("dom")
    sections = lax.axis_size("tm")
    places = sections // CORES
    me_time, me_dom = lax.axis_index("tm"), lax.axis_index("dom")
    core, place = me_time % CORES, me_time // CORES

    order = ring_order(parts)
    spot = [0] * parts
    for i, d in enumerate(order):
        spot[d] = i
    ahead = [(order[i], order[(i + 1) % parts]) for i in range(parts)]
    back = [(b, a) for a, b in ahead]
    my_spot = jnp.array(spot, jnp.int32)[me_dom]
    ring = jnp.array(order, jnp.int32)
    shifted = ring[(my_spot + jnp.arange(parts, dtype=jnp.int32)) % parts]
    info = jnp.concatenate([jnp.stack([core, place]).astype(jnp.int32), shifted])
    cols = tile_cols.reshape(-1)
    counts = tile_count.reshape(-1)

    own = [features[s] for s in range(snaps)]
    forward = [[x] for x in own]
    reverse = [[x] for x in own]
    far = parts // 2
    acc = spmm(info, cols, counts, tile_values, own, [(s, 2) for s in range(snaps)], None, False)
    for hop in range(1, far + 1):
        xs, pieces = [], []
        for s in range(snaps):
            if hop < far or s % 2 == 0:
                forward[s].append(lax.ppermute(forward[s][-1], "dom", ahead))
                xs.append(forward[s][-1])
                pieces.append((s, 2 + (parts - hop) % parts))
            if hop < far or s % 2 == 1:
                reverse[s].append(lax.ppermute(reverse[s][-1], "dom", back))
                xs.append(reverse[s][-1])
                pieces.append((s, 2 + hop))
        acc = spmm(info, cols, counts, tile_values, xs, pieces, acc, hop == far)
    keep_ax, send_ax = acc

    swap = [(t, t ^ 1) for t in range(sections)]
    other_ax = lax.ppermute(send_ax, "tm", swap)
    gx_own = gates(keep_ax, w_graph, w_input)
    gx_other = gates(other_ax, w_graph, w_input)

    bias = update_bias.reshape(1, -1)
    mine = nodes // CORES
    rows = mine // CHUNKS
    onward = [(t, t + CORES) for t in range(sections - CORES)]
    states = [
        lax.dynamic_slice_in_dim(hidden_start, core * mine + chunk * rows, rows, 0) for chunk in range(CHUNKS)
    ]
    hidden = [()] * CHUNKS
    for phase in range(places):
        for chunk in range(CHUNKS):
            state, keep, send = recurrence(
                info, states[chunk], gx_own, gx_other, w_hidden, bias, hidden[chunk], phase, chunk
            )
            hidden[chunk] = (keep, send)
            if phase < places - 1:
                states[chunk] = lax.ppermute(state, "tm", onward)
    swapped = [lax.ppermute(send, "tm", swap) for _, send in hidden]
    kept = jnp.concatenate([keep for keep, _ in hidden], axis=1)
    got = jnp.concatenate(swapped, axis=1)
    return jnp.where(
        core == 0, jnp.concatenate([kept, got], axis=1), jnp.concatenate([got, kept], axis=1)
    )


def solution(mesh):
    placed = (
        P("tm", "dom", None),
        P("tm", "dom", None, None, None, None),
        P("tm", "dom", None, None),
        P("tm", "dom", None),
        P("dom", None),
        P(),
        P(),
        P(),
        P(),
    )
    return jax.shard_map(
        per_device, mesh=mesh, in_specs=placed, out_specs=P("tm", "dom", None), check_vma=False
    )
```

```python
import functools

import jax
import jax.numpy as jnp
from jax import lax
from jax.experimental import pallas as pl
from jax.experimental.pallas import tpu as pltpu
from jax.sharding import PartitionSpec as P

BF16 = jnp.bfloat16
F32 = jnp.float32
CORES = 2
CHUNKS = 2
VMEM = pltpu.MemorySpace.VMEM
SMEM = pltpu.MemorySpace.SMEM


def ring_order(size):
    width = 1
    while width * width * 4 <= size:
        width *= 2
    depth = size // width
    walk = [(z, 0) for z in range(depth)]
    for step, z in enumerate(reversed(range(depth))):
        row = range(1, width) if step % 2 == 0 else reversed(range(1, width))
        walk += [(z, y) for y in row]
    return [z * width + y for z, y in walk]


def sigmoid(x):
    return 0.5 * jnp.tanh(0.5 * x) + 0.5


def params(mib=32):
    return pltpu.CompilerParams(vmem_limit_bytes=mib * 2**20)


def cost(flops, bytes_accessed):
    return pl.CostEstimate(flops=int(flops), bytes_accessed=int(bytes_accessed), transcendentals=0)


def where_am_i():
    me = lax.axis_index("tm")
    return lax.rem(me, CORES), lax.div(me, CORES)


def lookup(table, index):
    found = jnp.int32(table[0])
    for i, entry in enumerate(table[1:], 1):
        found = jnp.where(index == i, jnp.int32(entry), found)
    return found


def whole(memory=VMEM):
    return pl.BlockSpec(memory_space=memory)


def load_tiles(tiles, cols, counts, order):
    snaps, rows, parts, slots, blk, _ = tiles.shape
    half = rows // CORES
    spot = [0] * parts
    for i, d in enumerate(order):
        spot[d] = i

    def kernel(tiles, cols, counts, out, table, sems):
        core, _ = where_am_i()
        here = lookup(spot, lax.axis_index("dom"))
        parts_at = [lookup(order, lax.rem(here + step, parts)) for step in range(parts)]
        copies = []
        for snap in range(snaps):
            for step in range(parts):
                for h in range(CORES):
                    row = lax.rem(core + h, CORES) * half
                    copies.append(
                        pltpu.make_async_copy(
                            tiles.at[snap, pl.ds(row, half), parts_at[step]],
                            out.at[snap, pl.ds(h * half, half), step],
                            sems.at[snap, step, h],
                        )
                    )
                    copies[-1].start()

        def fill(at, carry):
            snap, rel = at // rows, at % rows
            row = lax.rem(rel + core * half, rows)
            for step in range(parts):
                count = counts[snap, row, parts_at[step]]
                for k in range(slots):
                    col = cols[snap, row, k, parts_at[step]]
                    table[(at * parts + step) * slots + k] = jnp.where(k < count, col, -1)
            return carry

        lax.fori_loop(0, snaps * rows, fill, 0)
        for copy in copies:
            copy.wait()

    return pl.pallas_call(
        kernel,
        out_shape=(
            jax.ShapeDtypeStruct(tiles.shape, tiles.dtype),
            jax.ShapeDtypeStruct((snaps * rows * parts * slots,), jnp.int32),
        ),
        in_specs=[whole(pltpu.MemorySpace.HBM), whole(SMEM), whole(SMEM)],
        out_specs=(whole(), whole(SMEM)),
        scratch_shapes=[pltpu.SemaphoreType.DMA((snaps, parts, CORES))],
        compiler_params=params(44),
        cost_estimate=cost(0, 2**20),
        name="load_tiles",
    )(tiles, jnp.swapaxes(cols, 2, 3), counts)


def picked(table, tiles, x_block, snap, rel, step, lhs, rhs):
    rows, parts, slots, blk = tiles.shape[1:5]
    for k in range(slots):
        col = table[((snap * rows + rel) * parts + step) * slots + k]
        block = x_block(pl.ds(pl.multiple_of(jnp.maximum(col, 0) * blk, blk), blk))
        rhs.append(jnp.where(col >= 0, block, jnp.zeros_like(block)))
        lhs.append(tiles[snap, rel, step, k])


def product(lhs, rhs):
    return jnp.dot(jnp.concatenate(lhs, axis=1), jnp.concatenate(rhs, axis=0), preferred_element_type=F32)


def spmm(table, tiles, xs, steps, acc, beside=()):
    snaps, rows, parts, slots, blk, _ = tiles.shape
    feats = xs[0].shape[-1]
    first = acc is None
    joint = xs[0].ndim == 3

    def kernel(table, tiles, *refs):
        x_refs, rest = refs[: len(xs)], refs[len(xs) :]
        out = rest[-1]
        for snap in range(snaps):
            for rel in range(rows):
                lhs, rhs = [], []
                for i, step in enumerate(steps):
                    x = x_refs[i].at[snap] if joint else x_refs[i * snaps + snap]
                    picked(table, tiles, lambda at: x[at, :], snap, rel, step, lhs, rhs)
                total = product(lhs, rhs)
                out[snap, rel] = total if first else total + rest[0][snap, rel]

    operands = [table, tiles, *xs] + ([] if first else [acc]) + list(beside)
    return pl.pallas_call(
        kernel,
        out_shape=jax.ShapeDtypeStruct((snaps, rows, blk, feats), F32),
        in_specs=[whole(SMEM)] + [whole()] * (len(operands) - 1),
        out_specs=whole(),
        compiler_params=params(),
        cost_estimate=cost(2 * len(steps) * snaps * rows * slots * blk * blk * feats * 4, 2**20),
        name="spmm",
    )(*operands)


def spmm_last(table, tiles, x, snap, step, acc):
    snaps, rows, parts, slots, blk, _ = tiles.shape
    feats = x.shape[-1]
    half = rows // CORES

    def kernel(table, tiles, x_ref, acc_in, *outs):
        for rel in range(rows):
            lhs, rhs = [], []
            picked(table, tiles, lambda at: x_ref[at, :], snap, rel, step, lhs, rhs)
            total = product(lhs, rhs) + acc_in[snap, rel]
            outs[rel // half][(rel % half) * blk : (rel % half + 1) * blk, :] = total.astype(BF16)

    part = jax.ShapeDtypeStruct((half * blk, feats), BF16)
    return pl.pallas_call(
        kernel,
        out_shape=(part, part),
        in_specs=[whole(SMEM)] + [whole()] * 3,
        out_specs=(whole(), whole()),
        compiler_params=params(),
        cost_estimate=cost(2 * rows * slots * blk * blk * feats * 4, 2**20),
        name="spmm_last",
    )(table, tiles, x, acc)


def write_gates(axs, w_graph, w_input, out):
    snaps, rows = len(axs), axs[0].shape[0]
    hid, width = w_input.shape
    graph = jnp.dot(jnp.concatenate(axs, axis=0), w_graph[...], preferred_element_type=F32)
    graph = jnp.maximum(graph, 0.0).astype(BF16)
    for j in range(0, width, hid):
        part = jnp.dot(graph, w_input[:, j : j + hid], preferred_element_type=F32)
        out[:, :, j : j + hid] = part.reshape(snaps, rows, hid)


def gates(axs, w_graph, w_input):
    snaps, rows = len(axs), axs[0].shape[0]
    hid, width = w_input.shape

    def kernel(*refs):
        write_gates([ref[...] for ref in refs[:snaps]], *refs[snaps:])

    return pl.pallas_call(
        kernel,
        out_shape=jax.ShapeDtypeStruct((snaps, rows, width), F32),
        in_specs=[whole()] * (snaps + 2),
        out_specs=whole(),
        compiler_params=params(),
        cost_estimate=cost(2 * snaps * rows * hid * width * 2, 2**20),
        name="gates",
    )(*axs, w_graph, w_input)


def run_steps(state, given_first, given_second, outs_first, outs_second, w_hidden, bias, state_out):
    hid = w_hidden.shape[0]
    block = min(256, hid)
    snaps = outs_first.shape[0]
    for step in range(CORES * snaps):
        s = step % snaps
        given, out = (given_first, outs_first) if step < snaps else (given_second, outs_second)
        low = state.astype(BF16)
        parts = []
        for j in range(0, hid, block):
            gh_r, gh_c, gh_u = (
                jnp.dot(low, w_hidden[:, g * hid + j : g * hid + j + block], preferred_element_type=F32)
                for g in (0, 2, 1)
            )
            gx_r, gx_u, gx_c = (given(s, slice(g * hid + j, g * hid + j + block)) for g in (0, 1, 2))
            reset = sigmoid(gx_r + gh_r)
            cand = jnp.tanh(gx_c + reset * gh_c)
            update = sigmoid(gx_u + gh_u + bias[:, j : j + block])
            parts.append(update * state[:, j : j + block] + (1.0 - update) * cand)
        state = jnp.concatenate(parts, axis=1)
        out[s] = state.astype(BF16)
    if state_out is not None:
        state_out[...] = state.astype(BF16)


def recurrence_first(hidden_start, gx_own, axs_other, w_graph, w_input, w_hidden, bias, chunk):
    snaps, mine, width = gx_own.shape
    feats, hid = w_graph.shape
    rows = mine // CHUNKS

    def kernel(hidden_start, gx_own, w_graph, w_input, w_hidden, bias, *refs):
        axs, (state_out, keep, send, gx_other) = refs[:snaps], refs[snaps:]
        core, place = where_am_i()
        at = slice(chunk * rows, (chunk + 1) * rows)
        write_gates([ref[at, :] for ref in axs], w_graph, w_input, gx_other)
        own = lambda s, columns: gx_own[s, at, columns]
        other = lambda s, columns: gx_other[s, :, columns]

        @pl.when((place == 0) & (core == 0))
        def _():
            state = hidden_start[chunk * rows : (chunk + 1) * rows, :]
            run_steps(state, own, other, keep, send, w_hidden, bias, state_out)

        @pl.when((place == 0) & (core != 0))
        def _():
            state = hidden_start[mine + chunk * rows : mine + (chunk + 1) * rows, :]
            run_steps(state, other, own, send, keep, w_hidden, bias, state_out)

    part = jax.ShapeDtypeStruct((snaps, rows, hid), BF16)
    return pl.pallas_call(
        kernel,
        out_shape=(
            jax.ShapeDtypeStruct((rows, hid), BF16),
            part,
            part,
            jax.ShapeDtypeStruct((snaps, rows, width), F32),
        ),
        in_specs=[whole()] * (6 + snaps),
        out_specs=(whole(),) * 4,
        compiler_params=params(),
        cost_estimate=cost(2 * CORES * snaps * rows * hid * 3 * hid * 4, 2**20),
        name="recurrence_first",
    )(hidden_start, gx_own, w_graph, w_input, w_hidden, bias, *axs_other)


def recurrence_later(state, gx_own, gx_other, w_hidden, bias, before, phase, chunk, last):
    snaps, rows, width = gx_other.shape
    hid = w_hidden.shape[0]

    def kernel(state_in, gx_own, gx_other, w_hidden, bias, keep_in, send_in, keep, send, state_out=None):
        core, place = where_am_i()
        at = slice(chunk * rows, (chunk + 1) * rows)
        own = lambda s, columns: gx_own[s, at, columns]
        other = lambda s, columns: gx_other[s, :, columns]

        @pl.when((place == phase) & (core == 0))
        def _():
            run_steps(state_in[...].astype(F32), own, other, keep, send, w_hidden, bias, state_out)

        @pl.when((place == phase) & (core != 0))
        def _():
            run_steps(state_in[...].astype(F32), other, own, send, keep, w_hidden, bias, state_out)

        @pl.when(place != phase)
        def _():
            keep[...] = keep_in[...]
            send[...] = send_in[...]

    part = jax.ShapeDtypeStruct((snaps, rows, hid), BF16)
    return pl.pallas_call(
        kernel,
        out_shape=(part, part) + (() if last else (jax.ShapeDtypeStruct((rows, hid), BF16),)),
        in_specs=[whole()] * 7,
        out_specs=(whole(),) * (2 if last else 3),
        compiler_params=params(),
        cost_estimate=cost(2 * CORES * snaps * rows * hid * 3 * hid * 4, 2**20),
        name="recurrence_later",
    )(state, gx_own, gx_other, w_hidden, bias, *before)


def write_out(out, pieces, nodes):
    snaps, rows, hid = pieces[0][0].shape
    shape = jax.ShapeDtypeStruct((snaps, nodes, hid), BF16)
    count = len(pieces)

    def kernel(*refs):
        sources, target, sems = refs[:count], refs[-2], refs[-1]
        core, _ = where_am_i()
        copies = []
        for i, (_, own, chunk) in enumerate(pieces):
            half = core if own else 1 - core
            start = pl.multiple_of(half * (nodes // CORES) + chunk * rows, rows)
            copies.append(pltpu.make_async_copy(sources[i], target.at[:, pl.ds(start, rows), :], sems.at[i]))
            copies[-1].start()
        for copy in copies:
            copy.wait()

    operands = [array for array, _, _ in pieces] + ([] if out is None else [out])
    return pl.pallas_call(
        kernel,
        out_shape=shape,
        in_specs=[whole()] * count + ([] if out is None else [whole(pl.ANY)]),
        out_specs=whole(pl.ANY),
        scratch_shapes=[pltpu.SemaphoreType.DMA((count,))],
        input_output_aliases={} if out is None else {count: 0},
        compiler_params=params(),
        cost_estimate=cost(0, 2**20),
        name="write_out",
    )(*operands)


def per_device(
    features, tile_values, tile_cols, tile_count, hidden_start, w_graph, w_input, w_hidden, update_bias
):
    snaps, nodes, feats = features.shape
    parts = lax.axis_size("dom")
    sections = lax.axis_size("tm")
    places = sections // CORES
    order = ring_order(parts)
    ahead = [(order[i], order[(i + 1) % parts]) for i in range(parts)]
    back = [(b, a) for a, b in ahead]

    far = parts // 2
    tiles, table = load_tiles(tile_values, tile_cols, tile_count, order)
    forward = lax.ppermute(features, "dom", ahead)
    reverse = lax.ppermute(features, "dom", back)
    forward, tiles, table = lax.optimization_barrier((forward, tiles, table))
    waiting = [([features, forward, reverse], [0, parts - 1, 1])]
    forward = [forward[s] for s in range(snaps)]
    reverse = [reverse[s] for s in range(snaps)]
    acc = None
    beside = [w_graph, w_input, w_hidden, hidden_start]
    for hop in range(2, far):
        for turn in range(2):
            for s in range(snaps):
                if s % 2 == turn:
                    forward[s] = lax.ppermute(forward[s], "dom", ahead)
                else:
                    reverse[s] = lax.ppermute(reverse[s], "dom", back)
        waiting.append((forward + reverse, [parts - hop, hop]))
        if hop > 2:
            acc = spmm(table, tiles, *waiting.pop(0), acc)
            first = [forward[s] if s % 2 == 0 else reverse[s] for s in range(snaps)]
            first, acc = lax.optimization_barrier((first, acc))
            forward = [first[s] if s % 2 == 0 else forward[s] for s in range(snaps)]
            reverse = [first[s] if s % 2 == 1 else reverse[s] for s in range(snaps)]
    arriving = [
        lax.ppermute(forward[s], "dom", ahead) if s % 2 == 0 else lax.ppermute(reverse[s], "dom", back)
        for s in range(snaps)
    ]
    while waiting:
        xs, steps = waiting.pop(0)
        acc = spmm(table, tiles, xs, steps, acc, [] if waiting else beside)
    swap = [(t, t ^ 1) for t in range(sections)]
    keep_ax, other_ax = [], []
    for s in range(snaps):
        keep, send = spmm_last(table, tiles, arriving[s], s, far, acc)
        keep_ax.append(keep)
        other_ax.append(lax.ppermute(send, "tm", swap))
    gx_own = gates(keep_ax, w_graph, w_input)

    bias = update_bias.reshape(1, -1)
    onward = [(t, t + CORES) for t in range(sections - CORES)]
    hidden, states, gx_other = [], [], []
    for chunk in range(CHUNKS):
        state, keep, send, gx = recurrence_first(
            hidden_start, gx_own, other_ax, w_graph, w_input, w_hidden, bias, chunk
        )
        hidden.append((keep, send))
        states.append(state)
        gx_other.append(gx)
    for phase in range(1, places):
        states = [lax.ppermute(state, "tm", onward) for state in states]
        for chunk in range(CHUNKS):
            last = phase == places - 1
            hidden[chunk] = recurrence_later(
                states[chunk], gx_own, gx_other[chunk], w_hidden, bias, hidden[chunk], phase, chunk, last
            )
            if not last:
                *hidden[chunk], states[chunk] = hidden[chunk]
    pieces = [(keep, True, chunk) for chunk, (keep, _) in enumerate(hidden)]
    pieces += [(lax.ppermute(send, "tm", swap), False, chunk) for chunk, (_, send) in enumerate(hidden)]
    out = write_out(None, pieces[:-1], nodes)
    return write_out(out, pieces[-1:], nodes)


def solution(mesh):
    placed = (
        P("tm", "dom", None),
        P("tm", "dom", None, None, None, None),
        P("tm", "dom", None, None),
        P("tm", "dom", None),
        P("dom", None),
        P(),
        P(),
        P(),
        P(),
    )
    return jax.shard_map(
        per_device, mesh=mesh, in_specs=placed, out_specs=P("tm", "dom", None), check_vma=False
    )
```

```python
import functools

import jax
import jax.numpy as jnp
from jax import lax
from jax.experimental import pallas as pl
from jax.experimental.pallas import tpu as pltpu
from jax.sharding import PartitionSpec as P

BF16 = jnp.bfloat16
F32 = jnp.float32
CORES = 2
CHUNKS = 2
VMEM = pltpu.MemorySpace.VMEM
SMEM = pltpu.MemorySpace.SMEM


def ring_order(size):
    width = 1
    while width * width * 4 <= size:
        width *= 2
    depth = size // width
    walk = [(z, 0) for z in range(depth)]
    for step, z in enumerate(reversed(range(depth))):
        row = range(1, width) if step % 2 == 0 else reversed(range(1, width))
        walk += [(z, y) for y in row]
    return [z * width + y for z, y in walk]


def sigmoid(x):
    return 0.5 * jnp.tanh(0.5 * x) + 0.5


def params(mib=32):
    return pltpu.CompilerParams(vmem_limit_bytes=mib * 2**20)


def cost(flops, bytes_accessed):
    return pl.CostEstimate(flops=int(flops), bytes_accessed=int(bytes_accessed), transcendentals=0)


def where_am_i():
    me = lax.axis_index("tm")
    return lax.rem(me, CORES), lax.div(me, CORES)


def lookup(table, index):
    found = jnp.int32(table[0])
    for i, entry in enumerate(table[1:], 1):
        found = jnp.where(index == i, jnp.int32(entry), found)
    return found


def whole(memory=VMEM):
    return pl.BlockSpec(memory_space=memory)


def load_tiles(tiles, cols, counts, order):
    snaps, rows, parts, slots, blk, _ = tiles.shape
    half = rows // CORES
    spot = [0] * parts
    for i, d in enumerate(order):
        spot[d] = i

    def kernel(tiles, cols, counts, out, table, sems):
        core, _ = where_am_i()
        here = lookup(spot, lax.axis_index("dom"))
        parts_at = [lookup(order, lax.rem(here + step, parts)) for step in range(parts)]
        copies = []
        for snap in range(snaps):
            for step in range(parts):
                for h in range(CORES):
                    row = lax.rem(core + h, CORES) * half
                    copies.append(
                        pltpu.make_async_copy(
                            tiles.at[snap, pl.ds(row, half), parts_at[step]],
                            out.at[snap, pl.ds(h * half, half), step],
                            sems.at[snap, step, h],
                        )
                    )
                    copies[-1].start()

        def fill(at, carry):
            snap, rel = at // rows, at % rows
            row = lax.rem(rel + core * half, rows)
            for step in range(parts):
                count = counts[snap, row, parts_at[step]]
                for k in range(slots):
                    col = cols[snap, row, k, parts_at[step]]
                    table[(at * parts + step) * slots + k] = jnp.where(k < count, col, -1)
            return carry

        lax.fori_loop(0, snaps * rows, fill, 0)
        for copy in copies:
            copy.wait()

    return pl.pallas_call(
        kernel,
        out_shape=(
            jax.ShapeDtypeStruct(tiles.shape, tiles.dtype),
            jax.ShapeDtypeStruct((snaps * rows * parts * slots,), jnp.int32),
        ),
        in_specs=[whole(pltpu.MemorySpace.HBM), whole(SMEM), whole(SMEM)],
        out_specs=(whole(), whole(SMEM)),
        scratch_shapes=[pltpu.SemaphoreType.DMA((snaps, parts, CORES))],
        compiler_params=params(44),
        cost_estimate=cost(0, 2**20),
        name="load_tiles",
    )(tiles, jnp.swapaxes(cols, 2, 3), counts)


def picked(table, tiles, x_block, snap, rel, step, lhs, rhs):
    rows, parts, slots, blk = tiles.shape[1:5]
    for k in range(slots):
        col = table[((snap * rows + rel) * parts + step) * slots + k]
        block = x_block(pl.ds(pl.multiple_of(jnp.maximum(col, 0) * blk, blk), blk))
        rhs.append(jnp.where(col >= 0, block, jnp.zeros_like(block)))
        lhs.append(tiles[snap, rel, step, k])


def product(lhs, rhs):
    return jnp.dot(jnp.concatenate(lhs, axis=1), jnp.concatenate(rhs, axis=0), preferred_element_type=F32)


def spmm(table, tiles, xs, steps, acc, beside=()):
    snaps, rows, parts, slots, blk, _ = tiles.shape
    feats = xs[0].shape[-1]
    first = acc is None
    joint = xs[0].ndim == 3

    def kernel(table, tiles, *refs):
        x_refs, rest = refs[: len(xs)], refs[len(xs) :]
        out = rest[-1]
        for snap in range(snaps):
            for rel in range(rows):
                lhs, rhs = [], []
                for i, step in enumerate(steps):
                    x = x_refs[i].at[snap] if joint else x_refs[i * snaps + snap]
                    picked(table, tiles, lambda at: x[at, :], snap, rel, step, lhs, rhs)
                total = product(lhs, rhs)
                out[snap, rel] = total if first else total + rest[0][snap, rel]

    operands = [table, tiles, *xs] + ([] if first else [acc]) + list(beside)
    return pl.pallas_call(
        kernel,
        out_shape=jax.ShapeDtypeStruct((snaps, rows, blk, feats), F32),
        in_specs=[whole(SMEM)] + [whole()] * (len(operands) - 1),
        out_specs=whole(),
        compiler_params=params(),
        cost_estimate=cost(2 * len(steps) * snaps * rows * slots * blk * blk * feats * 4, 2**20),
        name="spmm",
    )(*operands)


def spmm_last(table, tiles, x, snap, step, acc):
    snaps, rows, parts, slots, blk, _ = tiles.shape
    feats = x.shape[-1]
    half = rows // CORES

    def kernel(table, tiles, x_ref, acc_in, *outs):
        for rel in range(rows):
            lhs, rhs = [], []
            picked(table, tiles, lambda at: x_ref[at, :], snap, rel, step, lhs, rhs)
            total = product(lhs, rhs) + acc_in[snap, rel]
            outs[rel // half][(rel % half) * blk : (rel % half + 1) * blk, :] = total.astype(BF16)

    part = jax.ShapeDtypeStruct((half * blk, feats), BF16)
    return pl.pallas_call(
        kernel,
        out_shape=(part, part),
        in_specs=[whole(SMEM)] + [whole()] * 3,
        out_specs=(whole(), whole()),
        compiler_params=params(),
        cost_estimate=cost(2 * rows * slots * blk * blk * feats * 4, 2**20),
        name="spmm_last",
    )(table, tiles, x, acc)


def write_gates(axs, w_graph, w_input, out):
    snaps, rows = len(axs), axs[0].shape[0]
    hid, width = w_input.shape
    graph = jnp.dot(jnp.concatenate(axs, axis=0), w_graph[...], preferred_element_type=F32)
    graph = jnp.maximum(graph, 0.0).astype(BF16)
    for j in range(0, width, hid):
        part = jnp.dot(graph, w_input[:, j : j + hid], preferred_element_type=F32)
        out[:, :, j : j + hid] = part.reshape(snaps, rows, hid)


def gates(axs, w_graph, w_input):
    snaps, rows = len(axs), axs[0].shape[0]
    hid, width = w_input.shape

    def kernel(*refs):
        write_gates([ref[...] for ref in refs[:snaps]], *refs[snaps:])

    return pl.pallas_call(
        kernel,
        out_shape=jax.ShapeDtypeStruct((snaps, rows, width), F32),
        in_specs=[whole()] * (snaps + 2),
        out_specs=whole(),
        compiler_params=params(),
        cost_estimate=cost(2 * snaps * rows * hid * width * 2, 2**20),
        name="gates",
    )(*axs, w_graph, w_input)


def run_steps(state, given_first, given_second, outs_first, outs_second, w_hidden, bias, state_out):
    hid = w_hidden.shape[0]
    block = min(256, hid)
    snaps = outs_first.shape[0]
    for step in range(CORES * snaps):
        s = step % snaps
        given, out = (given_first, outs_first) if step < snaps else (given_second, outs_second)
        low = state.astype(BF16)
        parts = []
        for j in range(0, hid, block):
            gh_r, gh_c, gh_u = (
                jnp.dot(low, w_hidden[:, g * hid + j : g * hid + j + block], preferred_element_type=F32)
                for g in (0, 2, 1)
            )
            gx_r, gx_u, gx_c = (given(s, slice(g * hid + j, g * hid + j + block)) for g in (0, 1, 2))
            reset = sigmoid(gx_r + gh_r)
            cand = jnp.tanh(gx_c + reset * gh_c)
            update = sigmoid(gx_u + gh_u + bias[:, j : j + block])
            parts.append(update * state[:, j : j + block] + (1.0 - update) * cand)
        state = jnp.concatenate(parts, axis=1)
        out[s] = state.astype(BF16)
    if state_out is not None:
        state_out[...] = state.astype(BF16)


def recurrence_first(hidden_start, gx_own, axs_other, w_graph, w_input, w_hidden, bias, chunk):
    snaps, mine, width = gx_own.shape
    feats, hid = w_graph.shape
    rows = mine // CHUNKS

    def kernel(hidden_start, gx_own, w_graph, w_input, w_hidden, bias, *refs):
        axs, (state_out, keep, send, gx_other) = refs[:snaps], refs[snaps:]
        core, place = where_am_i()
        at = slice(chunk * rows, (chunk + 1) * rows)
        write_gates([ref[at, :] for ref in axs], w_graph, w_input, gx_other)
        own = lambda s, columns: gx_own[s, at, columns]
        other = lambda s, columns: gx_other[s, :, columns]

        @pl.when((place == 0) & (core == 0))
        def _():
            state = hidden_start[chunk * rows : (chunk + 1) * rows, :]
            run_steps(state, own, other, keep, send, w_hidden, bias, state_out)

        @pl.when((place == 0) & (core != 0))
        def _():
            state = hidden_start[mine + chunk * rows : mine + (chunk + 1) * rows, :]
            run_steps(state, other, own, send, keep, w_hidden, bias, state_out)

    part = jax.ShapeDtypeStruct((snaps, rows, hid), BF16)
    return pl.pallas_call(
        kernel,
        out_shape=(
            jax.ShapeDtypeStruct((rows, hid), BF16),
            part,
            part,
            jax.ShapeDtypeStruct((snaps, rows, width), F32),
        ),
        in_specs=[whole()] * (6 + snaps),
        out_specs=(whole(),) * 4,
        compiler_params=params(),
        cost_estimate=cost(2 * CORES * snaps * rows * hid * 3 * hid * 4, 2**20),
        name="recurrence_first",
    )(hidden_start, gx_own, w_graph, w_input, w_hidden, bias, *axs_other)


def recurrence_later(state, gx_own, gx_other, w_hidden, bias, before, phase, chunk, last):
    snaps, rows, width = gx_other.shape
    hid = w_hidden.shape[0]

    def kernel(state_in, gx_own, gx_other, w_hidden, bias, keep_in, send_in, keep, send, state_out=None):
        core, place = where_am_i()
        at = slice(chunk * rows, (chunk + 1) * rows)
        own = lambda s, columns: gx_own[s, at, columns]
        other = lambda s, columns: gx_other[s, :, columns]

        @pl.when((place == phase) & (core == 0))
        def _():
            run_steps(state_in[...].astype(F32), own, other, keep, send, w_hidden, bias, state_out)

        @pl.when((place == phase) & (core != 0))
        def _():
            run_steps(state_in[...].astype(F32), other, own, send, keep, w_hidden, bias, state_out)

        @pl.when(place != phase)
        def _():
            keep[...] = keep_in[...]
            send[...] = send_in[...]

    part = jax.ShapeDtypeStruct((snaps, rows, hid), BF16)
    return pl.pallas_call(
        kernel,
        out_shape=(part, part) + (() if last else (jax.ShapeDtypeStruct((rows, hid), BF16),)),
        in_specs=[whole()] * 7,
        out_specs=(whole(),) * (2 if last else 3),
        compiler_params=params(),
        cost_estimate=cost(2 * CORES * snaps * rows * hid * 3 * hid * 4, 2**20),
        name="recurrence_later",
    )(state, gx_own, gx_other, w_hidden, bias, *before)


def write_out(out, pieces, nodes):
    snaps, rows, hid = pieces[0][0].shape
    shape = jax.ShapeDtypeStruct((snaps, nodes, hid), BF16)
    count = len(pieces)

    def kernel(*refs):
        sources, target, sems = refs[:count], refs[-2], refs[-1]
        core, _ = where_am_i()
        copies = []
        for i, (_, own, chunk) in enumerate(pieces):
            half = core if own else 1 - core
            start = pl.multiple_of(half * (nodes // CORES) + chunk * rows, rows)
            copies.append(pltpu.make_async_copy(sources[i], target.at[:, pl.ds(start, rows), :], sems.at[i]))
            copies[-1].start()
        for copy in copies:
            copy.wait()

    operands = [array for array, _, _ in pieces] + ([] if out is None else [out])
    return pl.pallas_call(
        kernel,
        out_shape=shape,
        in_specs=[whole()] * count + ([] if out is None else [whole(pl.ANY)]),
        out_specs=whole(pl.ANY),
        scratch_shapes=[pltpu.SemaphoreType.DMA((count,))],
        input_output_aliases={} if out is None else {count: 0},
        compiler_params=params(),
        cost_estimate=cost(0, 2**20),
        name="write_out",
    )(*operands)


def per_device(
    features, tile_values, tile_cols, tile_count, hidden_start, w_graph, w_input, w_hidden, update_bias
):
    snaps, nodes, feats = features.shape
    parts = lax.axis_size("dom")
    sections = lax.axis_size("tm")
    places = sections // CORES
    order = ring_order(parts)
    ahead = [(order[i], order[(i + 1) % parts]) for i in range(parts)]
    back = [(b, a) for a, b in ahead]

    far = parts // 2
    tiles, table = load_tiles(tile_values, tile_cols, tile_count, order)
    forward = lax.ppermute(features, "dom", ahead)
    reverse = lax.ppermute(features, "dom", back)
    forward, tiles, table = lax.optimization_barrier((forward, tiles, table))
    waiting = [([features, forward, reverse], [0, parts - 1, 1])]
    forward = [forward[s] for s in range(snaps)]
    reverse = [reverse[s] for s in range(snaps)]
    acc = None
    beside = [w_graph, w_input, w_hidden, hidden_start]
    for hop in range(2, far):
        for turn in range(2):
            for s in range(snaps):
                if s % 2 == turn:
                    forward[s] = lax.ppermute(forward[s], "dom", ahead)
                else:
                    reverse[s] = lax.ppermute(reverse[s], "dom", back)
        waiting.append((forward + reverse, [parts - hop, hop]))
        if hop > 2:
            acc = spmm(table, tiles, *waiting.pop(0), acc)
            first = [forward[s] if s % 2 == 0 else reverse[s] for s in range(snaps)]
            first, acc = lax.optimization_barrier((first, acc))
            forward = [first[s] if s % 2 == 0 else forward[s] for s in range(snaps)]
            reverse = [first[s] if s % 2 == 1 else reverse[s] for s in range(snaps)]
    arriving = [
        lax.ppermute(forward[s], "dom", ahead) if s % 2 == 0 else lax.ppermute(reverse[s], "dom", back)
        for s in range(snaps)
    ]
    while waiting:
        xs, steps = waiting.pop(0)
        acc = spmm(table, tiles, xs, steps, acc, [] if waiting else beside)
    swap = [(t, t ^ 1) for t in range(sections)]
    keep_ax, other_ax = [], []
    for s in range(snaps):
        keep, send = spmm_last(table, tiles, arriving[s], s, far, acc)
        keep_ax.append(keep)
        other_ax.append(lax.ppermute(send, "tm", swap))
    gx_own = gates(keep_ax, w_graph, w_input)

    bias = update_bias.reshape(1, -1)
    onward = [(t, (t + CORES) % sections) for t in range(sections)]
    hidden, states, gx_other = [], [], []
    for chunk in range(CHUNKS):
        state, keep, send, gx = recurrence_first(
            hidden_start, gx_own, other_ax, w_graph, w_input, w_hidden, bias, chunk
        )
        hidden.append((keep, send))
        states.append(state)
        gx_other.append(gx)
    for phase in range(1, places):
        states = [lax.ppermute(state, "tm", onward) for state in states]
        for chunk in range(CHUNKS):
            last = phase == places - 1
            hidden[chunk] = recurrence_later(
                states[chunk], gx_own, gx_other[chunk], w_hidden, bias, hidden[chunk], phase, chunk, last
            )
            if not last:
                *hidden[chunk], states[chunk] = hidden[chunk]
    pieces = [(keep, True, chunk) for chunk, (keep, _) in enumerate(hidden)]
    pieces += [(lax.ppermute(send, "tm", swap), False, chunk) for chunk, (_, send) in enumerate(hidden)]
    out = write_out(None, pieces[:-1], nodes)
    return write_out(out, pieces[-1:], nodes)


def solution(mesh):
    placed = (
        P("tm", "dom", None),
        P("tm", "dom", None, None, None, None),
        P("tm", "dom", None, None),
        P("tm", "dom", None),
        P("dom", None),
        P(),
        P(),
        P(),
        P(),
    )
    return jax.shard_map(
        per_device, mesh=mesh, in_specs=placed, out_specs=P("tm", "dom", None), check_vma=False
    )
```

```python
import functools

import jax
import jax.numpy as jnp
from jax import lax
from jax.experimental import pallas as pl
from jax.experimental.pallas import tpu as pltpu
from jax.sharding import PartitionSpec as P

BF16 = jnp.bfloat16
F32 = jnp.float32
CORES = 2
CHUNKS = 2
VMEM = pltpu.MemorySpace.VMEM
SMEM = pltpu.MemorySpace.SMEM


def ring_order(size):
    width = 1
    while width * width * 4 <= size:
        width *= 2
    depth = size // width
    walk = [(z, 0) for z in range(depth)]
    for step, z in enumerate(reversed(range(depth))):
        row = range(1, width) if step % 2 == 0 else reversed(range(1, width))
        walk += [(z, y) for y in row]
    return [z * width + y for z, y in walk]


def sigmoid(x):
    return 0.5 * jnp.tanh(0.5 * x) + 0.5


def params(mib=32):
    return pltpu.CompilerParams(vmem_limit_bytes=mib * 2**20)


def cost(flops, bytes_accessed):
    return pl.CostEstimate(flops=int(flops), bytes_accessed=int(bytes_accessed), transcendentals=0)


def where_am_i():
    me = lax.axis_index("tm")
    return lax.rem(me, CORES), lax.div(me, CORES)


def lookup(table, index):
    found = jnp.int32(table[0])
    for i, entry in enumerate(table[1:], 1):
        found = jnp.where(index == i, jnp.int32(entry), found)
    return found


def whole(memory=VMEM):
    return pl.BlockSpec(memory_space=memory)


def load_tiles(tiles, cols, counts, order):
    snaps, rows, parts, slots, blk, _ = tiles.shape
    half = rows // CORES
    entries = snaps * rows * parts * slots
    spot = [0] * parts
    for i, d in enumerate(order):
        spot[d] = i
    slot = lax.broadcasted_iota(jnp.int32, (snaps, rows, slots, parts), 2)
    live = jnp.where(slot < counts[:, :, None, :], jnp.swapaxes(cols, 2, 3), -1)

    def kernel(tiles, live, out, table, sems):
        core, _ = where_am_i()
        copies = []
        for snap in range(snaps):
            for h in range(CORES):
                row = lax.rem(core + h, CORES) * half
                copies.append(
                    pltpu.make_async_copy(
                        tiles.at[snap, pl.ds(row, half)], out.at[snap, pl.ds(h * half, half)], sems.at[snap, h]
                    )
                )
                copies[-1].start()
        here = lookup(spot, lax.axis_index("dom"))
        parts_at = [lookup(order, lax.rem(here + step, parts)) for step in range(parts)]
        for step in range(parts):
            table[entries + step] = parts_at[step]

        def fill(at, carry):
            snap, rel = at // rows, at % rows
            row = lax.rem(rel + core * half, rows)
            for step in range(parts):
                for k in range(slots):
                    table[(at * parts + step) * slots + k] = live[snap, row, k, parts_at[step]]
            return carry

        lax.fori_loop(0, snaps * rows, fill, 0)
        for copy in copies:
            copy.wait()

    return pl.pallas_call(
        kernel,
        out_shape=(
            jax.ShapeDtypeStruct(tiles.shape, tiles.dtype),
            jax.ShapeDtypeStruct((entries + parts,), jnp.int32),
        ),
        in_specs=[whole(pltpu.MemorySpace.HBM), whole(SMEM)],
        out_specs=(whole(), whole(SMEM)),
        scratch_shapes=[pltpu.SemaphoreType.DMA((snaps, CORES))],
        compiler_params=params(44),
        cost_estimate=cost(0, 2**20),
        name="load_tiles",
    )(tiles, live)


def picked(table, tiles, x_block, snap, rel, step, lhs, rhs):
    snaps, rows, parts, slots, blk, _ = tiles.shape
    part = table[snaps * rows * parts * slots + step]
    for k in range(slots):
        col = table[((snap * rows + rel) * parts + step) * slots + k]
        block = x_block(pl.ds(pl.multiple_of(jnp.maximum(col, 0) * blk, blk), blk))
        rhs.append(jnp.where(col >= 0, block, jnp.zeros_like(block)))
        lhs.append(tiles[snap, rel, part, k])


def product(lhs, rhs):
    return jnp.dot(jnp.concatenate(lhs, axis=1), jnp.concatenate(rhs, axis=0), preferred_element_type=F32)


def spmm(table, tiles, xs, steps, acc, beside=()):
    snaps, rows, parts, slots, blk, _ = tiles.shape
    feats = xs[0].shape[-1]
    first = acc is None
    joint = xs[0].ndim == 3

    def kernel(table, tiles, *refs):
        x_refs, rest = refs[: len(xs)], refs[len(xs) :]
        out = rest[-1]
        for snap in range(snaps):
            for rel in range(rows):
                lhs, rhs = [], []
                for i, step in enumerate(steps):
                    x = x_refs[i].at[snap] if joint else x_refs[i * snaps + snap]
                    picked(table, tiles, lambda at: x[at, :], snap, rel, step, lhs, rhs)
                total = product(lhs, rhs)
                out[snap, rel] = total if first else total + rest[0][snap, rel]

    operands = [table, tiles, *xs] + ([] if first else [acc]) + list(beside)
    return pl.pallas_call(
        kernel,
        out_shape=jax.ShapeDtypeStruct((snaps, rows, blk, feats), F32),
        in_specs=[whole(SMEM)] + [whole()] * (len(operands) - 1),
        out_specs=whole(),
        compiler_params=params(),
        cost_estimate=cost(2 * len(steps) * snaps * rows * slots * blk * blk * feats * 4, 2**20),
        name="spmm",
    )(*operands)


def spmm_last(table, tiles, x, snap, step, acc):
    snaps, rows, parts, slots, blk, _ = tiles.shape
    feats = x.shape[-1]
    half = rows // CORES

    def kernel(table, tiles, x_ref, acc_in, *outs):
        for rel in range(rows):
            lhs, rhs = [], []
            picked(table, tiles, lambda at: x_ref[at, :], snap, rel, step, lhs, rhs)
            total = product(lhs, rhs) + acc_in[snap, rel]
            outs[rel // half][(rel % half) * blk : (rel % half + 1) * blk, :] = total.astype(BF16)

    part = jax.ShapeDtypeStruct((half * blk, feats), BF16)
    return pl.pallas_call(
        kernel,
        out_shape=(part, part),
        in_specs=[whole(SMEM)] + [whole()] * 3,
        out_specs=(whole(), whole()),
        compiler_params=params(),
        cost_estimate=cost(2 * rows * slots * blk * blk * feats * 4, 2**20),
        name="spmm_last",
    )(table, tiles, x, acc)


def write_gates(axs, w_graph, w_input, out):
    snaps, rows = len(axs), axs[0].shape[0]
    hid, width = w_input.shape
    graph = jnp.dot(jnp.concatenate(axs, axis=0), w_graph[...], preferred_element_type=F32)
    graph = jnp.maximum(graph, 0.0).astype(BF16)
    for j in range(0, width, hid):
        part = jnp.dot(graph, w_input[:, j : j + hid], preferred_element_type=F32)
        out[:, :, j : j + hid] = part.reshape(snaps, rows, hid)


def gates(axs, w_graph, w_input):
    snaps, rows = len(axs), axs[0].shape[0]
    hid, width = w_input.shape

    def kernel(*refs):
        write_gates([ref[...] for ref in refs[:snaps]], *refs[snaps:])

    return pl.pallas_call(
        kernel,
        out_shape=jax.ShapeDtypeStruct((snaps, rows, width), F32),
        in_specs=[whole()] * (snaps + 2),
        out_specs=whole(),
        compiler_params=params(),
        cost_estimate=cost(2 * snaps * rows * hid * width * 2, 2**20),
        name="gates",
    )(*axs, w_graph, w_input)


def run_steps(state, given_first, given_second, outs_first, outs_second, w_hidden, bias, state_out):
    hid = w_hidden.shape[0]
    block = min(256, hid)
    snaps = outs_first.shape[0]
    for step in range(CORES * snaps):
        s = step % snaps
        given, out = (given_first, outs_first) if step < snaps else (given_second, outs_second)
        low = state.astype(BF16)
        parts = []
        for j in range(0, hid, block):
            gh_r, gh_c, gh_u = (
                jnp.dot(low, w_hidden[:, g * hid + j : g * hid + j + block], preferred_element_type=F32)
                for g in (0, 2, 1)
            )
            gx_r, gx_u, gx_c = (given(s, slice(g * hid + j, g * hid + j + block)) for g in (0, 1, 2))
            reset = sigmoid(gx_r + gh_r)
            cand = jnp.tanh(gx_c + reset * gh_c)
            update = sigmoid(gx_u + gh_u + bias[:, j : j + block])
            parts.append(update * state[:, j : j + block] + (1.0 - update) * cand)
        state = jnp.concatenate(parts, axis=1)
        out[s] = state.astype(BF16)
    if state_out is not None:
        state_out[...] = state.astype(BF16)


def recurrence_first(hidden_start, gx_own, axs_other, w_graph, w_input, w_hidden, bias, chunk):
    snaps, mine, width = gx_own.shape
    feats, hid = w_graph.shape
    rows = mine // CHUNKS

    def kernel(hidden_start, gx_own, w_graph, w_input, w_hidden, bias, *refs):
        axs, (state_out, keep, send, gx_other) = refs[:snaps], refs[snaps:]
        core, place = where_am_i()
        at = slice(chunk * rows, (chunk + 1) * rows)
        write_gates([ref[at, :] for ref in axs], w_graph, w_input, gx_other)
        own = lambda s, columns: gx_own[s, at, columns]
        other = lambda s, columns: gx_other[s, :, columns]

        @pl.when((place == 0) & (core == 0))
        def _():
            state = hidden_start[chunk * rows : (chunk + 1) * rows, :]
            run_steps(state, own, other, keep, send, w_hidden, bias, state_out)

        @pl.when((place == 0) & (core != 0))
        def _():
            state = hidden_start[mine + chunk * rows : mine + (chunk + 1) * rows, :]
            run_steps(state, other, own, send, keep, w_hidden, bias, state_out)

    part = jax.ShapeDtypeStruct((snaps, rows, hid), BF16)
    return pl.pallas_call(
        kernel,
        out_shape=(
            jax.ShapeDtypeStruct((rows, hid), BF16),
            part,
            part,
            jax.ShapeDtypeStruct((snaps, rows, width), F32),
        ),
        in_specs=[whole()] * (6 + snaps),
        out_specs=(whole(),) * 4,
        compiler_params=params(),
        cost_estimate=cost(2 * CORES * snaps * rows * hid * 3 * hid * 4, 2**20),
        name="recurrence_first",
    )(hidden_start, gx_own, w_graph, w_input, w_hidden, bias, *axs_other)


def recurrence_later(state, gx_own, gx_other, w_hidden, bias, before, phase, chunk, last):
    snaps, rows, width = gx_other.shape
    hid = w_hidden.shape[0]

    def kernel(state_in, gx_own, gx_other, w_hidden, bias, keep_in, send_in, keep, send, state_out=None):
        core, place = where_am_i()
        at = slice(chunk * rows, (chunk + 1) * rows)
        own = lambda s, columns: gx_own[s, at, columns]
        other = lambda s, columns: gx_other[s, :, columns]

        @pl.when((place == phase) & (core == 0))
        def _():
            run_steps(state_in[...].astype(F32), own, other, keep, send, w_hidden, bias, state_out)

        @pl.when((place == phase) & (core != 0))
        def _():
            run_steps(state_in[...].astype(F32), other, own, send, keep, w_hidden, bias, state_out)

        @pl.when(place != phase)
        def _():
            keep[...] = keep_in[...]
            send[...] = send_in[...]

    part = jax.ShapeDtypeStruct((snaps, rows, hid), BF16)
    return pl.pallas_call(
        kernel,
        out_shape=(part, part) + (() if last else (jax.ShapeDtypeStruct((rows, hid), BF16),)),
        in_specs=[whole()] * 7,
        out_specs=(whole(),) * (2 if last else 3),
        compiler_params=params(),
        cost_estimate=cost(2 * CORES * snaps * rows * hid * 3 * hid * 4, 2**20),
        name="recurrence_later",
    )(state, gx_own, gx_other, w_hidden, bias, *before)


def write_out(out, pieces, nodes):
    snaps, rows, hid = pieces[0][0].shape
    shape = jax.ShapeDtypeStruct((snaps, nodes, hid), BF16)
    count = len(pieces)

    def kernel(*refs):
        sources, target, sems = refs[:count], refs[-2], refs[-1]
        core, _ = where_am_i()
        copies = []
        for i, (_, own, chunk) in enumerate(pieces):
            half = core if own else 1 - core
            start = pl.multiple_of(half * (nodes // CORES) + chunk * rows, rows)
            copies.append(pltpu.make_async_copy(sources[i], target.at[:, pl.ds(start, rows), :], sems.at[i]))
            copies[-1].start()
        for copy in copies:
            copy.wait()

    operands = [array for array, _, _ in pieces] + ([] if out is None else [out])
    return pl.pallas_call(
        kernel,
        out_shape=shape,
        in_specs=[whole()] * count + ([] if out is None else [whole(pl.ANY)]),
        out_specs=whole(pl.ANY),
        scratch_shapes=[pltpu.SemaphoreType.DMA((count,))],
        input_output_aliases={} if out is None else {count: 0},
        compiler_params=params(),
        cost_estimate=cost(0, 2**20),
        name="write_out",
    )(*operands)


def per_device(
    features, tile_values, tile_cols, tile_count, hidden_start, w_graph, w_input, w_hidden, update_bias
):
    snaps, nodes, feats = features.shape
    parts = lax.axis_size("dom")
    sections = lax.axis_size("tm")
    places = sections // CORES
    order = ring_order(parts)
    ahead = [(order[i], order[(i + 1) % parts]) for i in range(parts)]
    back = [(b, a) for a, b in ahead]

    far = parts // 2
    tiles, table = load_tiles(tile_values, tile_cols, tile_count, order)
    forward = lax.ppermute(features, "dom", ahead)
    reverse = lax.ppermute(features, "dom", back)
    forward, tiles, table = lax.optimization_barrier((forward, tiles, table))
    waiting = [([features, forward, reverse], [0, parts - 1, 1])]
    forward = [forward[s] for s in range(snaps)]
    reverse = [reverse[s] for s in range(snaps)]
    acc = None
    beside = [w_graph, w_input, w_hidden, hidden_start]
    for hop in range(2, far):
        for turn in range(2):
            for s in range(snaps):
                if s % 2 == turn:
                    forward[s] = lax.ppermute(forward[s], "dom", ahead)
                else:
                    reverse[s] = lax.ppermute(reverse[s], "dom", back)
        acc = spmm(table, tiles, *waiting.pop(0), acc)
        for s in range(snaps):
            passing = forward if s % 2 == 0 else reverse
            passing[s], acc = lax.optimization_barrier((passing[s], acc))
        waiting.append((forward + reverse, [parts - hop, hop]))
    arriving = [
        lax.ppermute(forward[s], "dom", ahead) if s % 2 == 0 else lax.ppermute(reverse[s], "dom", back)
        for s in range(snaps)
    ]
    while waiting:
        xs, steps = waiting.pop(0)
        acc = spmm(table, tiles, xs, steps, acc, [] if waiting else beside)
    swap = [(t, t ^ 1) for t in range(sections)]
    keep_ax, other_ax = [], []
    for s in range(snaps):
        keep, send = spmm_last(table, tiles, arriving[s], s, far, acc)
        keep_ax.append(keep)
        other_ax.append(lax.ppermute(send, "tm", swap))
    gx_own = gates(keep_ax, w_graph, w_input)

    bias = update_bias.reshape(1, -1)
    onward = [(t, (t + CORES) % sections) for t in range(sections)]
    hidden, states, gx_other = [], [], []
    for chunk in range(CHUNKS):
        state, keep, send, gx = recurrence_first(
            hidden_start, gx_own, other_ax, w_graph, w_input, w_hidden, bias, chunk
        )
        hidden.append((keep, send))
        states.append(state)
        gx_other.append(gx)
    for phase in range(1, places):
        states = [lax.ppermute(state, "tm", onward) for state in states]
        for chunk in range(CHUNKS):
            last = phase == places - 1
            hidden[chunk] = recurrence_later(
                states[chunk], gx_own, gx_other[chunk], w_hidden, bias, hidden[chunk], phase, chunk, last
            )
            if not last:
                *hidden[chunk], states[chunk] = hidden[chunk]
    pieces = [(keep, True, chunk) for chunk, (keep, _) in enumerate(hidden)]
    pieces += [(lax.ppermute(send, "tm", swap), False, chunk) for chunk, (_, send) in enumerate(hidden)]
    out = write_out(None, pieces[:-1], nodes)
    return write_out(out, pieces[-1:], nodes)


def solution(mesh):
    placed = (
        P("tm", "dom", None),
        P("tm", "dom", None, None, None, None),
        P("tm", "dom", None, None),
        P("tm", "dom", None),
        P("dom", None),
        P(),
        P(),
        P(),
        P(),
    )
    return jax.shard_map(
        per_device, mesh=mesh, in_specs=placed, out_specs=P("tm", "dom", None), check_vma=False
    )
```

```python
import functools

import jax
import jax.numpy as jnp
from jax import lax
from jax.experimental import pallas as pl
from jax.experimental.pallas import tpu as pltpu
from jax.sharding import PartitionSpec as P

BF16 = jnp.bfloat16
F32 = jnp.float32
CORES = 2
CHUNKS = 2
COVER_FLOPS = 3e9
VMEM = pltpu.MemorySpace.VMEM
SMEM = pltpu.MemorySpace.SMEM


def ring_order(size):
    width = 1
    while width * width * 4 <= size:
        width *= 2
    depth = size // width
    walk = [(z, 0) for z in range(depth)]
    for step, z in enumerate(reversed(range(depth))):
        row = range(1, width) if step % 2 == 0 else reversed(range(1, width))
        walk += [(z, y) for y in row]
    return [z * width + y for z, y in walk]


def sigmoid(x):
    return 0.5 * jnp.tanh(0.5 * x) + 0.5


def params(mib=32):
    return pltpu.CompilerParams(vmem_limit_bytes=mib * 2**20)


def cost(flops, bytes_accessed):
    return pl.CostEstimate(flops=int(flops), bytes_accessed=int(bytes_accessed), transcendentals=0)


def where_am_i():
    me = lax.axis_index("tm")
    return lax.rem(me, CORES), lax.div(me, CORES)


def lookup(table, index):
    found = jnp.int32(table[0])
    for i, entry in enumerate(table[1:], 1):
        found = jnp.where(index == i, jnp.int32(entry), found)
    return found


def whole(memory=VMEM):
    return pl.BlockSpec(memory_space=memory)


def column_table(tiles, cols, counts, order):
    snaps, rows, parts, slots, blk, _ = tiles.shape
    half = rows // CORES
    entries = snaps * rows * parts * slots
    spot = [0] * parts
    for i, d in enumerate(order):
        spot[d] = i
    slot = lax.broadcasted_iota(jnp.int32, (snaps, rows, slots, parts), 2)
    live = jnp.where(slot < counts[:, :, None, :], jnp.swapaxes(cols, 2, 3), -1)

    def kernel(live, table):
        core, _ = where_am_i()
        here = lookup(spot, lax.axis_index("dom"))
        parts_at = [lookup(order, lax.rem(here + step, parts)) for step in range(parts)]
        for step in range(parts):
            table[entries + step] = parts_at[step]
        for rel in range(rows):
            table[entries + parts + rel] = lax.rem(rel + core * half, rows)

        def fill(at, carry):
            snap, rel = at // rows, at % rows
            row = lax.rem(rel + core * half, rows)
            for step in range(parts):
                for k in range(slots):
                    table[(at * parts + step) * slots + k] = live[snap, row, k, parts_at[step]]
            return carry

        lax.fori_loop(0, snaps * rows, fill, 0)

    return pl.pallas_call(
        kernel,
        out_shape=jax.ShapeDtypeStruct((entries + parts + rows,), jnp.int32),
        in_specs=[whole(SMEM)],
        out_specs=whole(SMEM),
        compiler_params=params(),
        cost_estimate=cost(COVER_FLOPS, 2**20),
        name="column_table",
    )(live)


def picked(table, tiles, x_block, snap, rel, step, lhs, rhs):
    snaps, rows, parts, slots, blk, _ = tiles.shape
    part = table[snaps * rows * parts * slots + step]
    row = table[snaps * rows * parts * slots + parts + rel]
    for k in range(slots):
        col = table[((snap * rows + rel) * parts + step) * slots + k]
        block = x_block(pl.ds(pl.multiple_of(jnp.maximum(col, 0) * blk, blk), blk))
        rhs.append(jnp.where(col >= 0, block, jnp.zeros_like(block)))
        lhs.append(tiles[snap, row, part, k])


def product(lhs, rhs):
    return jnp.dot(jnp.concatenate(lhs, axis=1), jnp.concatenate(rhs, axis=0), preferred_element_type=F32)


def spmm(table, tiles, xs, steps, acc, beside=()):
    snaps, rows, parts, slots, blk, _ = tiles.shape
    feats = xs[0].shape[-1]
    first = acc is None
    joint = xs[0].ndim == 3

    def kernel(table, tiles, *refs):
        x_refs, rest = refs[: len(xs)], refs[len(xs) :]
        out = rest[-1]
        for snap in range(snaps):
            for rel in range(rows):
                lhs, rhs = [], []
                for i, step in enumerate(steps):
                    x = x_refs[i].at[snap] if joint else x_refs[i * snaps + snap]
                    picked(table, tiles, lambda at: x[at, :], snap, rel, step, lhs, rhs)
                total = product(lhs, rhs)
                out[snap, rel] = total if first else total + rest[0][snap, rel]

    operands = [table, tiles, *xs] + ([] if first else [acc]) + list(beside)
    return pl.pallas_call(
        kernel,
        out_shape=jax.ShapeDtypeStruct((snaps, rows, blk, feats), F32),
        in_specs=[whole(SMEM)] + [whole()] * (len(operands) - 1),
        out_specs=whole(),
        compiler_params=params(),
        cost_estimate=cost(2 * len(steps) * snaps * rows * slots * blk * blk * feats * 4, 2**20),
        name="spmm",
    )(*operands)


def dense_tiles(table, tiles, step):
    snaps, rows, parts, slots, blk, _ = tiles.shape

    def kernel(table, tiles, *outs):
        entries = snaps * rows * parts * slots
        part = table[entries + step]
        for snap in range(snaps):
            for rel in range(rows):
                row = table[entries + parts + rel]
                cols = [table[((snap * rows + rel) * parts + step) * slots + k] for k in range(slots)]
                found = [tiles[snap, row, part, k] for k in range(slots)]
                for c in range(rows):
                    terms = [jnp.where(col == c, tile, jnp.zeros_like(tile)) for col, tile in zip(cols, found)]
                    outs[snap][rel * blk : (rel + 1) * blk, c * blk : (c + 1) * blk] = functools.reduce(jnp.add, terms)

    out = jax.ShapeDtypeStruct((rows * blk, rows * blk), BF16)
    return pl.pallas_call(
        kernel,
        out_shape=(out,) * snaps,
        in_specs=[whole(SMEM), whole()],
        out_specs=(whole(),) * snaps,
        compiler_params=params(),
        cost_estimate=cost(0, 2**20),
        name="dense_tiles",
    )(table, tiles)


def spmm_last(dense, x, snap, acc):
    total_rows = dense.shape[0]
    feats = x.shape[-1]
    half = total_rows // CORES

    def kernel(dense, x, acc_in, keep, send):
        total = jnp.dot(dense[...], x[...], preferred_element_type=F32) + acc_in[snap].reshape(total_rows, feats)
        keep[...] = total[:half].astype(BF16)
        send[...] = total[half:].astype(BF16)

    part = jax.ShapeDtypeStruct((half, feats), BF16)
    return pl.pallas_call(
        kernel,
        out_shape=(part, part),
        in_specs=[whole()] * 3,
        out_specs=(whole(), whole()),
        compiler_params=params(),
        cost_estimate=cost(2 * total_rows * dense.shape[1] * feats, 2**20),
        name="spmm_last",
    )(dense, x, acc)


def write_gates(axs, w_graph, w_input, out):
    snaps, rows = len(axs), axs[0].shape[0]
    hid, width = w_input.shape
    graph = jnp.dot(jnp.concatenate(axs, axis=0), w_graph[...], preferred_element_type=F32)
    graph = jnp.maximum(graph, 0.0).astype(BF16)
    for j in range(0, width, hid):
        part = jnp.dot(graph, w_input[:, j : j + hid], preferred_element_type=F32)
        out[:, :, j : j + hid] = part.reshape(snaps, rows, hid)


def gates(axs, w_graph, w_input):
    snaps, rows = len(axs), axs[0].shape[0]
    hid, width = w_input.shape

    def kernel(*refs):
        write_gates([ref[...] for ref in refs[:snaps]], *refs[snaps:])

    return pl.pallas_call(
        kernel,
        out_shape=jax.ShapeDtypeStruct((snaps, rows, width), F32),
        in_specs=[whole()] * (snaps + 2),
        out_specs=whole(),
        compiler_params=params(),
        cost_estimate=cost(2 * snaps * rows * hid * width * 2, 2**20),
        name="gates",
    )(*axs, w_graph, w_input)


def run_steps(state, given_first, given_second, outs_first, outs_second, w_hidden, bias, state_out):
    hid = w_hidden.shape[0]
    block = min(256, hid)
    snaps = outs_first.shape[0]
    for step in range(CORES * snaps):
        s = step % snaps
        given, out = (given_first, outs_first) if step < snaps else (given_second, outs_second)
        low = state.astype(BF16)
        parts = []
        for j in range(0, hid, block):
            gh_r, gh_c, gh_u = (
                jnp.dot(low, w_hidden[:, g * hid + j : g * hid + j + block], preferred_element_type=F32)
                for g in (0, 2, 1)
            )
            gx_r, gx_u, gx_c = (given(s, slice(g * hid + j, g * hid + j + block)) for g in (0, 1, 2))
            reset = sigmoid(gx_r + gh_r)
            cand = jnp.tanh(gx_c + reset * gh_c)
            update = sigmoid(gx_u + gh_u + bias[:, j : j + block])
            parts.append(update * state[:, j : j + block] + (1.0 - update) * cand)
        state = jnp.concatenate(parts, axis=1)
        out[s] = state.astype(BF16)
    if state_out is not None:
        state_out[...] = state.astype(BF16)


def recurrence_first(hidden_start, gx_own, axs_other, w_graph, w_input, w_hidden, bias, chunk):
    snaps, mine, width = gx_own.shape
    feats, hid = w_graph.shape
    rows = mine // CHUNKS

    def kernel(hidden_start, gx_own, w_graph, w_input, w_hidden, bias, *refs):
        axs, (state_out, keep, send, gx_other) = refs[:snaps], refs[snaps:]
        core, place = where_am_i()
        at = slice(chunk * rows, (chunk + 1) * rows)
        write_gates([ref[at, :] for ref in axs], w_graph, w_input, gx_other)
        own = lambda s, columns: gx_own[s, at, columns]
        other = lambda s, columns: gx_other[s, :, columns]

        @pl.when((place == 0) & (core == 0))
        def _():
            state = hidden_start[chunk * rows : (chunk + 1) * rows, :]
            run_steps(state, own, other, keep, send, w_hidden, bias, state_out)

        @pl.when((place == 0) & (core != 0))
        def _():
            state = hidden_start[mine + chunk * rows : mine + (chunk + 1) * rows, :]
            run_steps(state, other, own, send, keep, w_hidden, bias, state_out)

    part = jax.ShapeDtypeStruct((snaps, rows, hid), BF16)
    return pl.pallas_call(
        kernel,
        out_shape=(
            jax.ShapeDtypeStruct((rows, hid), BF16),
            part,
            part,
            jax.ShapeDtypeStruct((snaps, rows, width), F32),
        ),
        in_specs=[whole()] * (6 + snaps),
        out_specs=(whole(),) * 4,
        compiler_params=params(),
        cost_estimate=cost(2 * CORES * snaps * rows * hid * 3 * hid * 4, 2**20),
        name="recurrence_first",
    )(hidden_start, gx_own, w_graph, w_input, w_hidden, bias, *axs_other)


def recurrence_later(state, gx_own, gx_other, w_hidden, bias, before, phase, chunk, last):
    snaps, rows, width = gx_other.shape
    hid = w_hidden.shape[0]

    def kernel(state_in, gx_own, gx_other, w_hidden, bias, keep_in, send_in, keep, send, state_out=None):
        core, place = where_am_i()
        at = slice(chunk * rows, (chunk + 1) * rows)
        own = lambda s, columns: gx_own[s, at, columns]
        other = lambda s, columns: gx_other[s, :, columns]

        @pl.when((place == phase) & (core == 0))
        def _():
            run_steps(state_in[...].astype(F32), own, other, keep, send, w_hidden, bias, state_out)

        @pl.when((place == phase) & (core != 0))
        def _():
            run_steps(state_in[...].astype(F32), other, own, send, keep, w_hidden, bias, state_out)

        @pl.when(place != phase)
        def _():
            keep[...] = keep_in[...]
            send[...] = send_in[...]

    part = jax.ShapeDtypeStruct((snaps, rows, hid), BF16)
    return pl.pallas_call(
        kernel,
        out_shape=(part, part) + (() if last else (jax.ShapeDtypeStruct((rows, hid), BF16),)),
        in_specs=[whole()] * 7,
        out_specs=(whole(),) * (2 if last else 3),
        compiler_params=params(),
        cost_estimate=cost(2 * CORES * snaps * rows * hid * 3 * hid * 4, 2**20),
        name="recurrence_later",
    )(state, gx_own, gx_other, w_hidden, bias, *before)


def write_out(out, pieces, nodes):
    snaps, rows, hid = pieces[0][0].shape
    shape = jax.ShapeDtypeStruct((snaps, nodes, hid), BF16)
    count = len(pieces)

    def kernel(*refs):
        sources, target, sems = refs[:count], refs[-2], refs[-1]
        core, _ = where_am_i()
        copies = []
        for i, (_, own, chunk) in enumerate(pieces):
            half = core if own else 1 - core
            start = pl.multiple_of(half * (nodes // CORES) + chunk * rows, rows)
            copies.append(pltpu.make_async_copy(sources[i], target.at[:, pl.ds(start, rows), :], sems.at[i]))
            copies[-1].start()
        for copy in copies:
            copy.wait()

    operands = [array for array, _, _ in pieces] + ([] if out is None else [out])
    return pl.pallas_call(
        kernel,
        out_shape=shape,
        in_specs=[whole()] * count + ([] if out is None else [whole(pl.ANY)]),
        out_specs=whole(pl.ANY),
        scratch_shapes=[pltpu.SemaphoreType.DMA((count,))],
        input_output_aliases={} if out is None else {count: 0},
        compiler_params=params(),
        cost_estimate=cost(0, 2**20),
        name="write_out",
    )(*operands)


def per_device(
    features, tile_values, tile_cols, tile_count, hidden_start, w_graph, w_input, w_hidden, update_bias
):
    snaps, nodes, feats = features.shape
    parts = lax.axis_size("dom")
    sections = lax.axis_size("tm")
    places = sections // CORES
    order = ring_order(parts)
    ahead = [(order[i], order[(i + 1) % parts]) for i in range(parts)]
    back = [(b, a) for a, b in ahead]

    far = parts // 2
    tiles = tile_values
    table = column_table(tile_values, tile_cols, tile_count, order)
    forward = lax.ppermute(features, "dom", ahead)
    reverse = lax.ppermute(features, "dom", back)
    acc = spmm(table, tiles, [features], [0], None)
    dense = dense_tiles(table, tiles, far)
    forward, acc, dense = lax.optimization_barrier((forward, acc, dense))
    waiting = [([forward, reverse], [parts - 1, 1])]
    forward = [forward[s] for s in range(snaps)]
    reverse = [reverse[s] for s in range(snaps)]
    beside = [w_graph, w_input, w_hidden, hidden_start]
    for hop in range(2, far):
        for turn in range(2):
            for s in range(snaps):
                if s % 2 == turn:
                    forward[s] = lax.ppermute(forward[s], "dom", ahead)
                else:
                    reverse[s] = lax.ppermute(reverse[s], "dom", back)
        acc = spmm(table, tiles, *waiting.pop(0), acc)
        for s in range(snaps):
            passing = forward if s % 2 == 0 else reverse
            passing[s], acc = lax.optimization_barrier((passing[s], acc))
        waiting.append((forward + reverse, [parts - hop, hop]))
    arriving = [
        lax.ppermute(forward[s], "dom", ahead) if s % 2 == 0 else lax.ppermute(reverse[s], "dom", back)
        for s in range(snaps)
    ]
    while waiting:
        xs, steps = waiting.pop(0)
        acc = spmm(table, tiles, xs, steps, acc, [] if waiting else beside)
    swap = [(t, t ^ 1) for t in range(sections)]
    keep_ax, other_ax = [], []
    for s in range(snaps):
        keep, send = spmm_last(dense[s], arriving[s], s, acc)
        keep_ax.append(keep)
        other_ax.append(lax.ppermute(send, "tm", swap))
    gx_own = gates(keep_ax, w_graph, w_input)

    bias = update_bias.reshape(1, -1)
    onward = [(t, (t + CORES) % sections) for t in range(sections)]
    hidden, states, gx_other = [], [], []
    for chunk in range(CHUNKS):
        state, keep, send, gx = recurrence_first(
            hidden_start, gx_own, other_ax, w_graph, w_input, w_hidden, bias, chunk
        )
        hidden.append((keep, send))
        states.append(state)
        gx_other.append(gx)
    for phase in range(1, places):
        states = [lax.ppermute(state, "tm", onward) for state in states]
        for chunk in range(CHUNKS):
            last = phase == places - 1
            hidden[chunk] = recurrence_later(
                states[chunk], gx_own, gx_other[chunk], w_hidden, bias, hidden[chunk], phase, chunk, last
            )
            if not last:
                *hidden[chunk], states[chunk] = hidden[chunk]
    pieces = [(keep, True, chunk) for chunk, (keep, _) in enumerate(hidden)]
    pieces += [(lax.ppermute(send, "tm", swap), False, chunk) for chunk, (_, send) in enumerate(hidden)]
    out = write_out(None, pieces[:-1], nodes)
    return write_out(out, pieces[-1:], nodes)


def solution(mesh):
    placed = (
        P("tm", "dom", None),
        P("tm", "dom", None, None, None, None),
        P("tm", "dom", None, None),
        P("tm", "dom", None),
        P("dom", None),
        P(),
        P(),
        P(),
        P(),
    )
    return jax.shard_map(
        per_device, mesh=mesh, in_specs=placed, out_specs=P("tm", "dom", None), check_vma=False
    )
```

```python
import functools

import jax
import jax.numpy as jnp
from jax import lax
from jax.experimental import pallas as pl
from jax.experimental.pallas import tpu as pltpu
from jax.sharding import PartitionSpec as P

BF16 = jnp.bfloat16
F32 = jnp.float32
CORES = 2
CHUNKS = 2
COVER_FLOPS = 3e9
VMEM = pltpu.MemorySpace.VMEM
SMEM = pltpu.MemorySpace.SMEM


def ring_order(size):
    width = 1
    while width * width * 4 <= size:
        width *= 2
    depth = size // width
    walk = [(z, 0) for z in range(depth)]
    for step, z in enumerate(reversed(range(depth))):
        row = range(1, width) if step % 2 == 0 else reversed(range(1, width))
        walk += [(z, y) for y in row]
    return [z * width + y for z, y in walk]


def sigmoid(x):
    return 0.5 * jnp.tanh(0.5 * x) + 0.5


def params(mib=32):
    return pltpu.CompilerParams(vmem_limit_bytes=mib * 2**20)


def cost(flops, bytes_accessed):
    return pl.CostEstimate(flops=int(flops), bytes_accessed=int(bytes_accessed), transcendentals=0)


def where_am_i():
    me = lax.axis_index("tm")
    return lax.rem(me, CORES), lax.div(me, CORES)


def lookup(table, index):
    found = jnp.int32(table[0])
    for i, entry in enumerate(table[1:], 1):
        found = jnp.where(index == i, jnp.int32(entry), found)
    return found


def whole(memory=VMEM):
    return pl.BlockSpec(memory_space=memory)


def column_table(tiles, cols, counts, order):
    snaps, rows, parts, slots, blk, _ = tiles.shape
    half = rows // CORES
    entries = snaps * rows * parts * slots
    spot = [0] * parts
    for i, d in enumerate(order):
        spot[d] = i
    slot = lax.broadcasted_iota(jnp.int32, (snaps, rows, slots, parts), 2)
    live = jnp.where(slot < counts[:, :, None, :], jnp.swapaxes(cols, 2, 3), -1)

    def kernel(live, table):
        core, _ = where_am_i()
        here = lookup(spot, lax.axis_index("dom"))
        parts_at = [lookup(order, lax.rem(here + step, parts)) for step in range(parts)]
        for step in range(parts):
            table[entries + step] = parts_at[step]
        for rel in range(rows):
            table[entries + parts + rel] = lax.rem(rel + core * half, rows)

        def fill(at, carry):
            snap, rel = at // rows, at % rows
            row = lax.rem(rel + core * half, rows)
            for step in range(parts):
                for k in range(slots):
                    table[(at * parts + step) * slots + k] = live[snap, row, k, parts_at[step]]
            return carry

        lax.fori_loop(0, snaps * rows, fill, 0)

    return pl.pallas_call(
        kernel,
        out_shape=jax.ShapeDtypeStruct((entries + parts + rows,), jnp.int32),
        in_specs=[whole(SMEM)],
        out_specs=whole(SMEM),
        compiler_params=params(),
        cost_estimate=cost(COVER_FLOPS, 2**20),
        name="column_table",
    )(live)


def picked(table, tiles, x_block, snap, rel, step, lhs, rhs):
    snaps, rows, parts, slots, blk, _ = tiles.shape
    part = table[snaps * rows * parts * slots + step]
    row = table[snaps * rows * parts * slots + parts + rel]
    for k in range(slots):
        col = table[((snap * rows + rel) * parts + step) * slots + k]
        block = x_block(pl.ds(pl.multiple_of(jnp.maximum(col, 0) * blk, blk), blk))
        rhs.append(jnp.where(col >= 0, block, jnp.zeros_like(block)))
        lhs.append(tiles[snap, row, part, k])


def product(lhs, rhs):
    return jnp.dot(jnp.concatenate(lhs, axis=1), jnp.concatenate(rhs, axis=0), preferred_element_type=F32)


def spmm(table, tiles, xs, steps, acc, beside=()):
    snaps, rows, parts, slots, blk, _ = tiles.shape
    feats = xs[0].shape[-1]
    first = acc is None
    joint = xs[0].ndim == 3

    def kernel(table, tiles, *refs):
        x_refs, rest = refs[: len(xs)], refs[len(xs) :]
        out = rest[-1]
        for snap in range(snaps):
            for rel in range(rows):
                lhs, rhs = [], []
                for i, step in enumerate(steps):
                    x = x_refs[i].at[snap] if joint else x_refs[i * snaps + snap]
                    picked(table, tiles, lambda at: x[at, :], snap, rel, step, lhs, rhs)
                total = product(lhs, rhs)
                out[snap, rel] = total if first else total + rest[0][snap, rel]

    operands = [table, tiles, *xs] + ([] if first else [acc]) + list(beside)
    return pl.pallas_call(
        kernel,
        out_shape=jax.ShapeDtypeStruct((snaps, rows, blk, feats), F32),
        in_specs=[whole(SMEM)] + [whole()] * (len(operands) - 1),
        out_specs=whole(),
        compiler_params=params(),
        cost_estimate=cost(2 * len(steps) * snaps * rows * slots * blk * blk * feats * 4, 2**20),
        name="spmm",
    )(*operands)


def dense_tiles(table, tiles, step):
    snaps, rows, parts, slots, blk, _ = tiles.shape

    def kernel(table, tiles, *outs):
        entries = snaps * rows * parts * slots
        part = table[entries + step]
        for snap in range(snaps):
            for rel in range(rows):
                row = table[entries + parts + rel]
                cols = [table[((snap * rows + rel) * parts + step) * slots + k] for k in range(slots)]
                found = [tiles[snap, row, part, k] for k in range(slots)]
                for c in range(rows):
                    terms = [jnp.where(col == c, tile, jnp.zeros_like(tile)) for col, tile in zip(cols, found)]
                    outs[snap][rel * blk : (rel + 1) * blk, c * blk : (c + 1) * blk] = functools.reduce(jnp.add, terms)

    out = jax.ShapeDtypeStruct((rows * blk, rows * blk), BF16)
    return pl.pallas_call(
        kernel,
        out_shape=(out,) * snaps,
        in_specs=[whole(SMEM), whole()],
        out_specs=(whole(),) * snaps,
        compiler_params=params(),
        cost_estimate=cost(0, 2**20),
        name="dense_tiles",
    )(table, tiles)


def spmm_last(dense, xs, acc):
    snaps = len(dense)
    total_rows = dense[0].shape[0]
    feats = xs[0].shape[-1]
    half = total_rows // CORES

    def kernel(*refs):
        mats, x_refs, (acc_in, keep, send) = refs[:snaps], refs[snaps : 2 * snaps], refs[2 * snaps :]
        for snap in range(snaps):
            total = jnp.dot(mats[snap][...], x_refs[snap][...], preferred_element_type=F32)
            total = total + acc_in[snap].reshape(total_rows, feats)
            keep[snap] = total[:half].astype(BF16)
            send[snap] = total[half:].astype(BF16)

    part = jax.ShapeDtypeStruct((snaps, half, feats), BF16)
    return pl.pallas_call(
        kernel,
        out_shape=(part, part),
        in_specs=[whole()] * (2 * snaps + 1),
        out_specs=(whole(), whole()),
        compiler_params=params(),
        cost_estimate=cost(2 * snaps * total_rows * dense[0].shape[1] * feats, 2**20),
        name="spmm_last",
    )(*dense, *xs, acc)


def write_gates(ax, w_graph, w_input, out):
    snaps, rows, feats = ax.shape
    hid, width = w_input.shape
    graph = jnp.dot(ax.reshape(snaps * rows, feats), w_graph[...], preferred_element_type=F32)
    graph = jnp.maximum(graph, 0.0).astype(BF16)
    for j in range(0, width, hid):
        part = jnp.dot(graph, w_input[:, j : j + hid], preferred_element_type=F32)
        out[:, :, j : j + hid] = part.reshape(snaps, rows, hid)


def gates(ax, w_graph, w_input):
    snaps, rows, _ = ax.shape
    hid, width = w_input.shape

    def kernel(ax, *refs):
        write_gates(ax[...], *refs)

    return pl.pallas_call(
        kernel,
        out_shape=jax.ShapeDtypeStruct((snaps, rows, width), F32),
        in_specs=[whole()] * 3,
        out_specs=whole(),
        compiler_params=params(),
        cost_estimate=cost(2 * snaps * rows * hid * width * 2, 2**20),
        name="gates",
    )(ax, w_graph, w_input)


def run_steps(state, given_first, given_second, outs_first, outs_second, w_hidden, bias, state_out):
    hid = w_hidden.shape[0]
    block = min(256, hid)
    snaps = outs_first.shape[0]
    for step in range(CORES * snaps):
        s = step % snaps
        given, out = (given_first, outs_first) if step < snaps else (given_second, outs_second)
        low = state.astype(BF16)
        parts = []
        for j in range(0, hid, block):
            gh_r, gh_c, gh_u = (
                jnp.dot(low, w_hidden[:, g * hid + j : g * hid + j + block], preferred_element_type=F32)
                for g in (0, 2, 1)
            )
            gx_r, gx_u, gx_c = (given(s, slice(g * hid + j, g * hid + j + block)) for g in (0, 1, 2))
            reset = sigmoid(gx_r + gh_r)
            cand = jnp.tanh(gx_c + reset * gh_c)
            update = sigmoid(gx_u + gh_u + bias[:, j : j + block])
            parts.append(update * state[:, j : j + block] + (1.0 - update) * cand)
        state = jnp.concatenate(parts, axis=1)
        out[s] = state.astype(BF16)
    if state_out is not None:
        state_out[...] = state.astype(BF16)


def recurrence_first(hidden_start, gx_own, ax_other, w_graph, w_input, w_hidden, bias, chunk):
    snaps, mine, width = gx_own.shape
    feats, hid = w_graph.shape
    rows = mine // CHUNKS

    def kernel(hidden_start, gx_own, ax_other, w_graph, w_input, w_hidden, bias, state_out, keep, send, gx_other):
        core, place = where_am_i()
        at = slice(chunk * rows, (chunk + 1) * rows)
        write_gates(ax_other[:, at, :], w_graph, w_input, gx_other)
        own = lambda s, columns: gx_own[s, at, columns]
        other = lambda s, columns: gx_other[s, :, columns]

        @pl.when((place == 0) & (core == 0))
        def _():
            state = hidden_start[chunk * rows : (chunk + 1) * rows, :]
            run_steps(state, own, other, keep, send, w_hidden, bias, state_out)

        @pl.when((place == 0) & (core != 0))
        def _():
            state = hidden_start[mine + chunk * rows : mine + (chunk + 1) * rows, :]
            run_steps(state, other, own, send, keep, w_hidden, bias, state_out)

    part = jax.ShapeDtypeStruct((snaps, rows, hid), BF16)
    return pl.pallas_call(
        kernel,
        out_shape=(
            jax.ShapeDtypeStruct((rows, hid), BF16),
            part,
            part,
            jax.ShapeDtypeStruct((snaps, rows, width), F32),
        ),
        in_specs=[whole()] * 7,
        out_specs=(whole(),) * 4,
        compiler_params=params(),
        cost_estimate=cost(2 * CORES * snaps * rows * hid * 3 * hid * 4, 2**20),
        name="recurrence_first",
    )(hidden_start, gx_own, ax_other, w_graph, w_input, w_hidden, bias)


def recurrence_later(state, gx_own, gx_other, w_hidden, bias, before, phase, chunk, last):
    snaps, rows, width = gx_other.shape
    hid = w_hidden.shape[0]

    def kernel(state_in, gx_own, gx_other, w_hidden, bias, keep_in, send_in, keep, send, state_out=None):
        core, place = where_am_i()
        at = slice(chunk * rows, (chunk + 1) * rows)
        own = lambda s, columns: gx_own[s, at, columns]
        other = lambda s, columns: gx_other[s, :, columns]

        @pl.when((place == phase) & (core == 0))
        def _():
            run_steps(state_in[...].astype(F32), own, other, keep, send, w_hidden, bias, state_out)

        @pl.when((place == phase) & (core != 0))
        def _():
            run_steps(state_in[...].astype(F32), other, own, send, keep, w_hidden, bias, state_out)

        @pl.when(place != phase)
        def _():
            keep[...] = keep_in[...]
            send[...] = send_in[...]

    part = jax.ShapeDtypeStruct((snaps, rows, hid), BF16)
    return pl.pallas_call(
        kernel,
        out_shape=(part, part) + (() if last else (jax.ShapeDtypeStruct((rows, hid), BF16),)),
        in_specs=[whole()] * 7,
        out_specs=(whole(),) * (2 if last else 3),
        compiler_params=params(),
        cost_estimate=cost(2 * CORES * snaps * rows * hid * 3 * hid * 4, 2**20),
        name="recurrence_later",
    )(state, gx_own, gx_other, w_hidden, bias, *before)


def write_out(out, pieces, nodes):
    snaps, rows, hid = pieces[0][0].shape
    shape = jax.ShapeDtypeStruct((snaps, nodes, hid), BF16)
    count = len(pieces)

    def kernel(*refs):
        sources, target, sems = refs[:count], refs[-2], refs[-1]
        core, _ = where_am_i()
        copies = []
        for i, (_, own, chunk) in enumerate(pieces):
            half = core if own else 1 - core
            start = pl.multiple_of(half * (nodes // CORES) + chunk * rows, rows)
            copies.append(pltpu.make_async_copy(sources[i], target.at[:, pl.ds(start, rows), :], sems.at[i]))
            copies[-1].start()
        for copy in copies:
            copy.wait()

    operands = [array for array, _, _ in pieces] + ([] if out is None else [out])
    return pl.pallas_call(
        kernel,
        out_shape=shape,
        in_specs=[whole()] * count + ([] if out is None else [whole(pl.ANY)]),
        out_specs=whole(pl.ANY),
        scratch_shapes=[pltpu.SemaphoreType.DMA((count,))],
        input_output_aliases={} if out is None else {count: 0},
        compiler_params=params(),
        cost_estimate=cost(0, 2**20),
        name="write_out",
    )(*operands)


def per_device(
    features, tile_values, tile_cols, tile_count, hidden_start, w_graph, w_input, w_hidden, update_bias
):
    snaps, nodes, feats = features.shape
    parts = lax.axis_size("dom")
    sections = lax.axis_size("tm")
    places = sections // CORES
    order = ring_order(parts)
    ahead = [(order[i], order[(i + 1) % parts]) for i in range(parts)]
    back = [(b, a) for a, b in ahead]

    far = parts // 2
    tiles = tile_values
    table = column_table(tile_values, tile_cols, tile_count, order)
    forward = lax.ppermute(features, "dom", ahead)
    reverse = lax.ppermute(features, "dom", back)
    acc = spmm(table, tiles, [features], [0], None)
    dense = dense_tiles(table, tiles, far)
    forward, acc, dense = lax.optimization_barrier((forward, acc, dense))
    waiting = [([forward, reverse], [parts - 1, 1])]
    forward = [forward[s] for s in range(snaps)]
    reverse = [reverse[s] for s in range(snaps)]
    beside = [w_graph, w_input, w_hidden, hidden_start]
    for hop in range(2, far):
        for turn in range(2):
            for s in range(snaps):
                if s % 2 == turn:
                    forward[s] = lax.ppermute(forward[s], "dom", ahead)
                else:
                    reverse[s] = lax.ppermute(reverse[s], "dom", back)
        acc = spmm(table, tiles, *waiting.pop(0), acc)
        for s in range(snaps):
            passing = forward if s % 2 == 0 else reverse
            passing[s], acc = lax.optimization_barrier((passing[s], acc))
        waiting.append((forward + reverse, [parts - hop, hop]))
    arriving = [
        lax.ppermute(forward[s], "dom", ahead) if s % 2 == 0 else lax.ppermute(reverse[s], "dom", back)
        for s in range(snaps)
    ]
    while waiting:
        xs, steps = waiting.pop(0)
        acc = spmm(table, tiles, xs, steps, acc, [] if waiting else beside)
    swap = [(t, t ^ 1) for t in range(sections)]
    keep_ax, send_ax = spmm_last(dense, arriving, acc)
    other_ax = lax.ppermute(send_ax, "tm", swap)
    gx_own = gates(keep_ax, w_graph, w_input)

    bias = update_bias.reshape(1, -1)
    onward = [(t, (t + CORES) % sections) for t in range(sections)]
    hidden, states, gx_other = [], [], []
    for chunk in range(CHUNKS):
        state, keep, send, gx = recurrence_first(
            hidden_start, gx_own, other_ax, w_graph, w_input, w_hidden, bias, chunk
        )
        hidden.append((keep, send))
        states.append(state)
        gx_other.append(gx)
    for phase in range(1, places):
        states = [lax.ppermute(state, "tm", onward) for state in states]
        for chunk in range(CHUNKS):
            last = phase == places - 1
            hidden[chunk] = recurrence_later(
                states[chunk], gx_own, gx_other[chunk], w_hidden, bias, hidden[chunk], phase, chunk, last
            )
            if not last:
                *hidden[chunk], states[chunk] = hidden[chunk]
    pieces = [(keep, True, chunk) for chunk, (keep, _) in enumerate(hidden)]
    pieces += [(lax.ppermute(send, "tm", swap), False, chunk) for chunk, (_, send) in enumerate(hidden)]
    out = write_out(None, pieces[:-1], nodes)
    return write_out(out, pieces[-1:], nodes)


def solution(mesh):
    placed = (
        P("tm", "dom", None),
        P("tm", "dom", None, None, None, None),
        P("tm", "dom", None, None),
        P("tm", "dom", None),
        P("dom", None),
        P(),
        P(),
        P(),
        P(),
    )
    return jax.shard_map(
        per_device, mesh=mesh, in_specs=placed, out_specs=P("tm", "dom", None), check_vma=False
    )
```

```python
import functools

import jax
import jax.numpy as jnp
from jax import lax
from jax.experimental import pallas as pl
from jax.experimental.pallas import tpu as pltpu
from jax.sharding import PartitionSpec as P

BF16 = jnp.bfloat16
F32 = jnp.float32
CORES = 2
CHUNKS = 2
COVER_FLOPS = 3e9
VMEM = pltpu.MemorySpace.VMEM
SMEM = pltpu.MemorySpace.SMEM


def ring_order(size):
    width = 1
    while width * width * 4 <= size:
        width *= 2
    depth = size // width
    walk = [(z, 0) for z in range(depth)]
    for step, z in enumerate(reversed(range(depth))):
        row = range(1, width) if step % 2 == 0 else reversed(range(1, width))
        walk += [(z, y) for y in row]
    return [z * width + y for z, y in walk]


def sigmoid(x):
    return 0.5 * jnp.tanh(0.5 * x) + 0.5


def params(mib=32):
    return pltpu.CompilerParams(vmem_limit_bytes=mib * 2**20)


def cost(flops, bytes_accessed):
    return pl.CostEstimate(flops=int(flops), bytes_accessed=int(bytes_accessed), transcendentals=0)


def where_am_i():
    me = lax.axis_index("tm")
    return lax.rem(me, CORES), lax.div(me, CORES)


def lookup(table, index):
    found = jnp.int32(table[0])
    for i, entry in enumerate(table[1:], 1):
        found = jnp.where(index == i, jnp.int32(entry), found)
    return found


def whole(memory=VMEM):
    return pl.BlockSpec(memory_space=memory)


def column_table(tiles, cols, counts, order):
    snaps, rows, parts, slots, blk, _ = tiles.shape
    half = rows // CORES
    entries = snaps * rows * parts * slots
    spot = [0] * parts
    for i, d in enumerate(order):
        spot[d] = i
    slot = lax.broadcasted_iota(jnp.int32, (snaps, rows, slots, parts), 2)
    live = jnp.where(slot < counts[:, :, None, :], jnp.swapaxes(cols, 2, 3), -1)

    def kernel(live, table):
        core, _ = where_am_i()
        here = lookup(spot, lax.axis_index("dom"))
        parts_at = [lookup(order, lax.rem(here + step, parts)) for step in range(parts)]
        for step in range(parts):
            table[entries + step] = parts_at[step]
        for rel in range(rows):
            table[entries + parts + rel] = lax.rem(rel + core * half, rows)

        def fill(at, carry):
            snap, rel = at // rows, at % rows
            row = lax.rem(rel + core * half, rows)
            for step in range(parts):
                for k in range(slots):
                    table[(at * parts + step) * slots + k] = live[snap, row, k, parts_at[step]]
            return carry

        lax.fori_loop(0, snaps * rows, fill, 0)

    return pl.pallas_call(
        kernel,
        out_shape=jax.ShapeDtypeStruct((entries + parts + rows,), jnp.int32),
        in_specs=[whole(SMEM)],
        out_specs=whole(SMEM),
        compiler_params=params(),
        cost_estimate=cost(COVER_FLOPS, 2**20),
        name="column_table",
    )(live)


def picked(table, tiles, x_block, snap, rel, step, lhs, rhs):
    snaps, rows, parts, slots, blk, _ = tiles.shape
    part = table[snaps * rows * parts * slots + step]
    row = table[snaps * rows * parts * slots + parts + rel]
    for k in range(slots):
        col = table[((snap * rows + rel) * parts + step) * slots + k]
        block = x_block(pl.ds(pl.multiple_of(jnp.maximum(col, 0) * blk, blk), blk))
        rhs.append(jnp.where(col >= 0, block, jnp.zeros_like(block)))
        lhs.append(tiles[snap, row, part, k])


def product(lhs, rhs):
    return jnp.dot(jnp.concatenate(lhs, axis=1), jnp.concatenate(rhs, axis=0), preferred_element_type=F32)


def spmm(table, tiles, xs, steps, acc, beside=()):
    snaps, rows, parts, slots, blk, _ = tiles.shape
    feats = xs[0].shape[-1]
    first = acc is None
    joint = xs[0].ndim == 3

    def kernel(table, tiles, *refs):
        x_refs, rest = refs[: len(xs)], refs[len(xs) :]
        out = rest[-1]
        for snap in range(snaps):
            for rel in range(rows):
                lhs, rhs = [], []
                for i, step in enumerate(steps):
                    x = x_refs[i].at[snap] if joint else x_refs[i * snaps + snap]
                    picked(table, tiles, lambda at: x[at, :], snap, rel, step, lhs, rhs)
                total = product(lhs, rhs)
                out[snap, rel] = total if first else total + rest[0][snap, rel]

    operands = [table, tiles, *xs] + ([] if first else [acc]) + list(beside)
    return pl.pallas_call(
        kernel,
        out_shape=jax.ShapeDtypeStruct((snaps, rows, blk, feats), F32),
        in_specs=[whole(SMEM)] + [whole()] * (len(operands) - 1),
        out_specs=whole(),
        compiler_params=params(),
        cost_estimate=cost(2 * len(steps) * snaps * rows * slots * blk * blk * feats * 4, 2**20),
        name="spmm",
    )(*operands)


def dense_tiles(table, tiles, step):
    snaps, rows, parts, slots, blk, _ = tiles.shape

    def kernel(table, tiles, *outs):
        entries = snaps * rows * parts * slots
        part = table[entries + step]
        for snap in range(snaps):
            for rel in range(rows):
                row = table[entries + parts + rel]
                cols = [table[((snap * rows + rel) * parts + step) * slots + k] for k in range(slots)]
                found = [tiles[snap, row, part, k] for k in range(slots)]
                for c in range(rows):
                    terms = [jnp.where(col == c, tile, jnp.zeros_like(tile)) for col, tile in zip(cols, found)]
                    outs[snap][rel * blk : (rel + 1) * blk, c * blk : (c + 1) * blk] = functools.reduce(jnp.add, terms)

    out = jax.ShapeDtypeStruct((rows * blk, rows * blk), BF16)
    return pl.pallas_call(
        kernel,
        out_shape=(out,) * snaps,
        in_specs=[whole(SMEM), whole()],
        out_specs=(whole(),) * snaps,
        compiler_params=params(),
        cost_estimate=cost(0, 2**20),
        name="dense_tiles",
    )(table, tiles)


def spmm_last(dense, xs, acc):
    snaps = len(dense)
    total_rows = dense[0].shape[0]
    feats = xs[0].shape[-1]
    half = total_rows // CORES

    def kernel(*refs):
        mats, x_refs, (acc_in, keep, send) = refs[:snaps], refs[snaps : 2 * snaps], refs[2 * snaps :]
        for snap in range(snaps):
            total = jnp.dot(mats[snap][...], x_refs[snap][...], preferred_element_type=F32)
            total = total + acc_in[snap].reshape(total_rows, feats)
            keep[snap] = total[:half].astype(BF16)
            send[snap] = total[half:].astype(BF16)

    part = jax.ShapeDtypeStruct((snaps, half, feats), BF16)
    return pl.pallas_call(
        kernel,
        out_shape=(part, part),
        in_specs=[whole()] * (2 * snaps + 1),
        out_specs=(whole(), whole()),
        compiler_params=params(),
        cost_estimate=cost(2 * snaps * total_rows * dense[0].shape[1] * feats, 2**20),
        name="spmm_last",
    )(*dense, *xs, acc)


def write_gates(ax, w_graph, w_input, out):
    snaps, rows, feats = ax.shape
    hid, width = w_input.shape
    graph = jnp.dot(ax.reshape(snaps * rows, feats), w_graph[...], preferred_element_type=F32)
    graph = jnp.maximum(graph, 0.0).astype(BF16)
    for j in range(0, width, hid):
        part = jnp.dot(graph, w_input[:, j : j + hid], preferred_element_type=F32)
        out[:, :, j : j + hid] = part.reshape(snaps, rows, hid)


def gates(ax, w_graph, w_input):
    snaps, rows, _ = ax.shape
    hid, width = w_input.shape

    def kernel(ax, *refs):
        write_gates(ax[...], *refs)

    return pl.pallas_call(
        kernel,
        out_shape=jax.ShapeDtypeStruct((snaps, rows, width), F32),
        in_specs=[whole()] * 3,
        out_specs=whole(),
        compiler_params=params(),
        cost_estimate=cost(2 * snaps * rows * hid * width * 2, 2**20),
        name="gates",
    )(ax, w_graph, w_input)


def run_steps(state, given_first, given_second, outs_first, outs_second, w_hidden, bias, state_out):
    hid = w_hidden.shape[0]
    block = min(256, hid)
    snaps = outs_first.shape[0]
    for step in range(CORES * snaps):
        s = step % snaps
        given, out = (given_first, outs_first) if step < snaps else (given_second, outs_second)
        low = state.astype(BF16)
        parts = []
        for j in range(0, hid, block):
            gh_r, gh_c, gh_u = (
                jnp.dot(low, w_hidden[:, g * hid + j : g * hid + j + block], preferred_element_type=F32)
                for g in (0, 2, 1)
            )
            gx_r, gx_u, gx_c = (given(s, slice(g * hid + j, g * hid + j + block)) for g in (0, 1, 2))
            reset = sigmoid(gx_r + gh_r)
            cand = jnp.tanh(gx_c + reset * gh_c)
            update = sigmoid(gx_u + gh_u + bias[:, j : j + block])
            parts.append(update * state[:, j : j + block] + (1.0 - update) * cand)
        state = jnp.concatenate(parts, axis=1)
        out[s] = state.astype(BF16)
    if state_out is not None:
        state_out[...] = state.astype(BF16)


def recurrence_first(hidden_start, gx_own, ax_other, w_graph, w_input, w_hidden, bias, chunk):
    snaps, mine, width = gx_own.shape
    feats, hid = w_graph.shape
    rows = mine // CHUNKS

    def kernel(hidden_start, gx_own, ax_other, w_graph, w_input, w_hidden, bias, state_out, keep, send, gx_other):
        core, place = where_am_i()
        at = slice(chunk * rows, (chunk + 1) * rows)
        write_gates(ax_other[:, at, :], w_graph, w_input, gx_other)
        own = lambda s, columns: gx_own[s, at, columns]
        other = lambda s, columns: gx_other[s, :, columns]

        @pl.when((place == 0) & (core == 0))
        def _():
            state = hidden_start[chunk * rows : (chunk + 1) * rows, :]
            run_steps(state, own, other, keep, send, w_hidden, bias, state_out)

        @pl.when((place == 0) & (core != 0))
        def _():
            state = hidden_start[mine + chunk * rows : mine + (chunk + 1) * rows, :]
            run_steps(state, other, own, send, keep, w_hidden, bias, state_out)

    part = jax.ShapeDtypeStruct((snaps, rows, hid), BF16)
    return pl.pallas_call(
        kernel,
        out_shape=(
            jax.ShapeDtypeStruct((rows, hid), BF16),
            part,
            part,
            jax.ShapeDtypeStruct((snaps, rows, width), F32),
        ),
        in_specs=[whole()] * 7,
        out_specs=(whole(),) * 4,
        compiler_params=params(),
        cost_estimate=cost(2 * CORES * snaps * rows * hid * 3 * hid * 4, 2**20),
        name="recurrence_first",
    )(hidden_start, gx_own, ax_other, w_graph, w_input, w_hidden, bias)


def recurrence_later(state, gx_own, gx_other, w_hidden, bias, before, phase, chunk, last):
    snaps, rows, width = gx_other.shape
    hid = w_hidden.shape[0]

    def kernel(state_in, gx_own, gx_other, w_hidden, bias, keep_in, send_in, keep, send, state_out=None):
        core, place = where_am_i()
        at = slice(chunk * rows, (chunk + 1) * rows)
        own = lambda s, columns: gx_own[s, at, columns]
        other = lambda s, columns: gx_other[s, :, columns]

        @pl.when((place == phase) & (core == 0))
        def _():
            run_steps(state_in[...].astype(F32), own, other, keep, send, w_hidden, bias, state_out)

        @pl.when((place == phase) & (core != 0))
        def _():
            run_steps(state_in[...].astype(F32), other, own, send, keep, w_hidden, bias, state_out)

        @pl.when(place != phase)
        def _():
            keep[...] = keep_in[...]
            send[...] = send_in[...]

    part = jax.ShapeDtypeStruct((snaps, rows, hid), BF16)
    return pl.pallas_call(
        kernel,
        out_shape=(part, part) + (() if last else (jax.ShapeDtypeStruct((rows, hid), BF16),)),
        in_specs=[whole()] * 7,
        out_specs=(whole(),) * (2 if last else 3),
        compiler_params=params(),
        cost_estimate=cost(2 * CORES * snaps * rows * hid * 3 * hid * 4, 2**20),
        name="recurrence_later",
    )(state, gx_own, gx_other, w_hidden, bias, *before)


def write_out(out, pieces, nodes):
    snaps, rows, hid = pieces[0][0].shape
    shape = jax.ShapeDtypeStruct((snaps, nodes, hid), BF16)
    count = len(pieces)

    def kernel(*refs):
        sources, target, sems = refs[:count], refs[-2], refs[-1]
        core, _ = where_am_i()
        copies = []
        for i, (_, own, chunk) in enumerate(pieces):
            half = core if own else 1 - core
            start = pl.multiple_of(half * (nodes // CORES) + chunk * rows, rows)
            copies.append(pltpu.make_async_copy(sources[i], target.at[:, pl.ds(start, rows), :], sems.at[i]))
            copies[-1].start()
        for copy in copies:
            copy.wait()

    operands = [array for array, _, _ in pieces] + ([] if out is None else [out])
    return pl.pallas_call(
        kernel,
        out_shape=shape,
        in_specs=[whole()] * count + ([] if out is None else [whole(pl.ANY)]),
        out_specs=whole(pl.ANY),
        scratch_shapes=[pltpu.SemaphoreType.DMA((count,))],
        input_output_aliases={} if out is None else {count: 0},
        compiler_params=params(),
        cost_estimate=cost(0, 2**20),
        name="write_out",
    )(*operands)


def per_device(
    features, tile_values, tile_cols, tile_count, hidden_start, w_graph, w_input, w_hidden, update_bias
):
    snaps, nodes, feats = features.shape
    parts = lax.axis_size("dom")
    sections = lax.axis_size("tm")
    places = sections // CORES
    order = ring_order(parts)
    ahead = [(order[i], order[(i + 1) % parts]) for i in range(parts)]
    back = [(b, a) for a, b in ahead]

    far = parts // 2
    tiles = tile_values
    table = column_table(tile_values, tile_cols, tile_count, order)
    forward = lax.ppermute(features, "dom", ahead)
    reverse = lax.ppermute(features, "dom", back)
    acc = spmm(table, tiles, [features], [0], None)
    dense = dense_tiles(table, tiles, far)
    forward, acc, dense = lax.optimization_barrier((forward, acc, dense))
    waiting = [([forward, reverse], [parts - 1, 1])]
    forward = [forward[s] for s in range(snaps)]
    reverse = [reverse[s] for s in range(snaps)]
    beside = [w_graph, w_input, w_hidden, hidden_start]
    for hop in range(2, far):
        for turn in range(2):
            for s in range(snaps):
                if s % 2 == turn:
                    forward[s] = lax.ppermute(forward[s], "dom", ahead)
                else:
                    reverse[s] = lax.ppermute(reverse[s], "dom", back)
        if hop < far - 1:
            acc = spmm(table, tiles, *waiting.pop(0), acc)
            for s in range(snaps):
                passing = forward if s % 2 == 0 else reverse
                passing[s], acc = lax.optimization_barrier((passing[s], acc))
        waiting.append((forward + reverse, [parts - hop, hop]))
    arriving = [
        lax.ppermute(forward[s], "dom", ahead) if s % 2 == 0 else lax.ppermute(reverse[s], "dom", back)
        for s in range(snaps)
    ]
    while waiting:
        xs, steps = waiting.pop(0)
        acc = spmm(table, tiles, xs, steps, acc, [] if waiting else beside)
    swap = [(t, t ^ 1) for t in range(sections)]
    keep_ax, send_ax = spmm_last(dense, arriving, acc)
    other_ax = lax.ppermute(send_ax, "tm", swap)
    gx_own = gates(keep_ax, w_graph, w_input)

    bias = update_bias.reshape(1, -1)
    onward = [(t, (t + CORES) % sections) for t in range(sections)]
    hidden, states, gx_other = [], [], []
    for chunk in range(CHUNKS):
        state, keep, send, gx = recurrence_first(
            hidden_start, gx_own, other_ax, w_graph, w_input, w_hidden, bias, chunk
        )
        hidden.append((keep, send))
        states.append(state)
        gx_other.append(gx)
    for phase in range(1, places):
        states = [lax.ppermute(state, "tm", onward) for state in states]
        for chunk in range(CHUNKS):
            last = phase == places - 1
            hidden[chunk] = recurrence_later(
                states[chunk], gx_own, gx_other[chunk], w_hidden, bias, hidden[chunk], phase, chunk, last
            )
            if not last:
                *hidden[chunk], states[chunk] = hidden[chunk]
    pieces = [(keep, True, chunk) for chunk, (keep, _) in enumerate(hidden)]
    pieces += [(lax.ppermute(send, "tm", swap), False, chunk) for chunk, (_, send) in enumerate(hidden)]
    out = write_out(None, pieces[:-1], nodes)
    return write_out(out, pieces[-1:], nodes)


def solution(mesh):
    placed = (
        P("tm", "dom", None),
        P("tm", "dom", None, None, None, None),
        P("tm", "dom", None, None),
        P("tm", "dom", None),
        P("dom", None),
        P(),
        P(),
        P(),
        P(),
    )
    return jax.shard_map(
        per_device, mesh=mesh, in_specs=placed, out_specs=P("tm", "dom", None), check_vma=False
    )
```

```python
import functools

import jax
import jax.numpy as jnp
from jax import lax
from jax.experimental import pallas as pl
from jax.experimental.pallas import tpu as pltpu
from jax.sharding import PartitionSpec as P

BF16 = jnp.bfloat16
F32 = jnp.float32
CORES = 2
CHUNKS = 2
COVER_FLOPS = 3e9
VMEM = pltpu.MemorySpace.VMEM
SMEM = pltpu.MemorySpace.SMEM


def ring_order(size):
    width = 1
    while width * width * 4 <= size:
        width *= 2
    depth = size // width
    walk = [(z, 0) for z in range(depth)]
    for step, z in enumerate(reversed(range(depth))):
        row = range(1, width) if step % 2 == 0 else reversed(range(1, width))
        walk += [(z, y) for y in row]
    return [z * width + y for z, y in walk]


def sigmoid(x):
    return 0.5 * jnp.tanh(0.5 * x) + 0.5


def params(mib=32):
    return pltpu.CompilerParams(vmem_limit_bytes=mib * 2**20)


def cost(flops, bytes_accessed):
    return pl.CostEstimate(flops=int(flops), bytes_accessed=int(bytes_accessed), transcendentals=0)


def where_am_i():
    me = lax.axis_index("tm")
    return lax.rem(me, CORES), lax.div(me, CORES)


def lookup(table, index):
    found = jnp.int32(table[0])
    for i, entry in enumerate(table[1:], 1):
        found = jnp.where(index == i, jnp.int32(entry), found)
    return found


def whole(memory=VMEM):
    return pl.BlockSpec(memory_space=memory)


def column_table(tiles, cols, counts, order):
    snaps, rows, parts, slots, blk, _ = tiles.shape
    half = rows // CORES
    entries = snaps * rows * parts * slots
    spot = [0] * parts
    for i, d in enumerate(order):
        spot[d] = i
    slot = lax.broadcasted_iota(jnp.int32, (snaps, rows, slots, parts), 2)
    live = jnp.where(slot < counts[:, :, None, :], jnp.swapaxes(cols, 2, 3), -1)

    def kernel(live, table):
        core, _ = where_am_i()
        here = lookup(spot, lax.axis_index("dom"))
        parts_at = [lookup(order, lax.rem(here + step, parts)) for step in range(parts)]
        for step in range(parts):
            table[entries + step] = parts_at[step]
        for rel in range(rows):
            table[entries + parts + rel] = lax.rem(rel + core * half, rows)

        def fill(at, carry):
            snap, rel = at // rows, at % rows
            row = lax.rem(rel + core * half, rows)
            for step in range(parts):
                for k in range(slots):
                    table[(at * parts + step) * slots + k] = live[snap, row, k, parts_at[step]]
            return carry

        lax.fori_loop(0, snaps * rows, fill, 0)

    return pl.pallas_call(
        kernel,
        out_shape=jax.ShapeDtypeStruct((entries + parts + rows,), jnp.int32),
        in_specs=[whole(SMEM)],
        out_specs=whole(SMEM),
        compiler_params=params(),
        cost_estimate=cost(COVER_FLOPS, 2**20),
        name="column_table",
    )(live)


def picked(table, tiles, x_block, snap, rel, step, lhs, rhs):
    snaps, rows, parts, slots, blk, _ = tiles.shape
    part = table[snaps * rows * parts * slots + step]
    row = table[snaps * rows * parts * slots + parts + rel]
    for k in range(slots):
        col = table[((snap * rows + rel) * parts + step) * slots + k]
        block = x_block(pl.ds(pl.multiple_of(jnp.maximum(col, 0) * blk, blk), blk))
        rhs.append(jnp.where(col >= 0, block, jnp.zeros_like(block)))
        lhs.append(tiles[snap, row, part, k])


def product(lhs, rhs):
    return jnp.dot(jnp.concatenate(lhs, axis=1), jnp.concatenate(rhs, axis=0), preferred_element_type=F32)


def spmm(table, tiles, xs, steps, acc, beside=()):
    snaps, rows, parts, slots, blk, _ = tiles.shape
    feats = xs[0].shape[-1]
    first = acc is None
    joint = xs[0].ndim == 3

    def kernel(table, tiles, *refs):
        x_refs, rest = refs[: len(xs)], refs[len(xs) :]
        out = rest[-1]
        for snap in range(snaps):
            for rel in range(rows):
                lhs, rhs = [], []
                for i, step in enumerate(steps):
                    x = x_refs[i].at[snap] if joint else x_refs[i * snaps + snap]
                    picked(table, tiles, lambda at: x[at, :], snap, rel, step, lhs, rhs)
                total = product(lhs, rhs)
                out[snap, rel] = total if first else total + rest[0][snap, rel]

    operands = [table, tiles, *xs] + ([] if first else [acc]) + list(beside)
    return pl.pallas_call(
        kernel,
        out_shape=jax.ShapeDtypeStruct((snaps, rows, blk, feats), F32),
        in_specs=[whole(SMEM)] + [whole()] * (len(operands) - 1),
        out_specs=whole(),
        compiler_params=params(),
        cost_estimate=cost(2 * len(steps) * snaps * rows * slots * blk * blk * feats * 4, 2**20),
        name="spmm",
    )(*operands)


def dense_tiles(table, tiles, step):
    snaps, rows, parts, slots, blk, _ = tiles.shape

    def kernel(table, tiles, *outs):
        entries = snaps * rows * parts * slots
        part = table[entries + step]
        for snap in range(snaps):
            for rel in range(rows):
                row = table[entries + parts + rel]
                cols = [table[((snap * rows + rel) * parts + step) * slots + k] for k in range(slots)]
                found = [tiles[snap, row, part, k] for k in range(slots)]
                for c in range(rows):
                    terms = [jnp.where(col == c, tile, jnp.zeros_like(tile)) for col, tile in zip(cols, found)]
                    outs[snap][rel * blk : (rel + 1) * blk, c * blk : (c + 1) * blk] = functools.reduce(jnp.add, terms)

    out = jax.ShapeDtypeStruct((rows * blk, rows * blk), BF16)
    return pl.pallas_call(
        kernel,
        out_shape=(out,) * snaps,
        in_specs=[whole(SMEM), whole()],
        out_specs=(whole(),) * snaps,
        compiler_params=params(),
        cost_estimate=cost(0, 2**20),
        name="dense_tiles",
    )(table, tiles)


def spmm_last(dense, xs, acc):
    snaps = len(dense)
    total_rows = dense[0].shape[0]
    feats = xs[0].shape[-1]
    half = total_rows // CORES

    def kernel(*refs):
        mats, x_refs, (acc_in, keep, send) = refs[:snaps], refs[snaps : 2 * snaps], refs[2 * snaps :]
        for snap in range(snaps):
            total = jnp.dot(mats[snap][...], x_refs[snap][...], preferred_element_type=F32)
            total = total + acc_in[snap].reshape(total_rows, feats)
            keep[snap] = total[:half].astype(BF16)
            send[snap] = total[half:].astype(BF16)

    part = jax.ShapeDtypeStruct((snaps, half, feats), BF16)
    return pl.pallas_call(
        kernel,
        out_shape=(part, part),
        in_specs=[whole()] * (2 * snaps + 1),
        out_specs=(whole(), whole()),
        compiler_params=params(),
        cost_estimate=cost(2 * snaps * total_rows * dense[0].shape[1] * feats, 2**20),
        name="spmm_last",
    )(*dense, *xs, acc)


def write_gates(ax, w_graph, w_input, out):
    snaps, rows, feats = ax.shape
    hid, width = w_input.shape
    graph = jnp.dot(ax.reshape(snaps * rows, feats), w_graph[...], preferred_element_type=F32)
    graph = jnp.maximum(graph, 0.0).astype(BF16)
    for j in range(0, width, hid):
        part = jnp.dot(graph, w_input[:, j : j + hid], preferred_element_type=F32)
        out[:, :, j : j + hid] = part.reshape(snaps, rows, hid)


def gates(ax, w_graph, w_input):
    snaps, rows, _ = ax.shape
    hid, width = w_input.shape

    def kernel(ax, *refs):
        write_gates(ax[...], *refs)

    return pl.pallas_call(
        kernel,
        out_shape=jax.ShapeDtypeStruct((snaps, rows, width), F32),
        in_specs=[whole()] * 3,
        out_specs=whole(),
        compiler_params=params(),
        cost_estimate=cost(2 * snaps * rows * hid * width * 2, 2**20),
        name="gates",
    )(ax, w_graph, w_input)


def run_steps(state, given_first, given_second, outs_first, outs_second, w_hidden, bias, state_out):
    hid = w_hidden.shape[0]
    block = min(256, hid)
    snaps = outs_first.shape[0]
    for step in range(CORES * snaps):
        s = step % snaps
        given, out = (given_first, outs_first) if step < snaps else (given_second, outs_second)
        low = state.astype(BF16)
        parts = []
        for j in range(0, hid, block):
            gh_r, gh_c, gh_u = (
                jnp.dot(low, w_hidden[:, g * hid + j : g * hid + j + block], preferred_element_type=F32)
                for g in (0, 2, 1)
            )
            gx_r, gx_u, gx_c = (given(s, slice(g * hid + j, g * hid + j + block)) for g in (0, 1, 2))
            reset = sigmoid(gx_r + gh_r)
            cand = jnp.tanh(gx_c + reset * gh_c)
            update = sigmoid(gx_u + gh_u + bias[:, j : j + block])
            parts.append(update * state[:, j : j + block] + (1.0 - update) * cand)
        state = jnp.concatenate(parts, axis=1)
        out[s] = state.astype(BF16)
    if state_out is not None:
        state_out[...] = state.astype(BF16)


def recurrence_first(hidden_start, gx_own, ax_other, w_graph, w_input, w_hidden, bias, chunk):
    snaps, mine, width = gx_own.shape
    feats, hid = w_graph.shape
    rows = mine // CHUNKS

    def kernel(hidden_start, gx_own, ax_other, w_graph, w_input, w_hidden, bias, state_out, keep, send, gx_other):
        core, place = where_am_i()
        at = slice(chunk * rows, (chunk + 1) * rows)
        write_gates(ax_other[:, at, :], w_graph, w_input, gx_other)
        own = lambda s, columns: gx_own[s, at, columns]
        other = lambda s, columns: gx_other[s, :, columns]

        @pl.when((place == 0) & (core == 0))
        def _():
            state = hidden_start[chunk * rows : (chunk + 1) * rows, :]
            run_steps(state, own, other, keep, send, w_hidden, bias, state_out)

        @pl.when((place == 0) & (core != 0))
        def _():
            state = hidden_start[mine + chunk * rows : mine + (chunk + 1) * rows, :]
            run_steps(state, other, own, send, keep, w_hidden, bias, state_out)

    part = jax.ShapeDtypeStruct((snaps, rows, hid), BF16)
    return pl.pallas_call(
        kernel,
        out_shape=(
            jax.ShapeDtypeStruct((rows, hid), BF16),
            part,
            part,
            jax.ShapeDtypeStruct((snaps, rows, width), F32),
        ),
        in_specs=[whole()] * 7,
        out_specs=(whole(),) * 4,
        compiler_params=params(),
        cost_estimate=cost(2 * CORES * snaps * rows * hid * 3 * hid * 4, 2**20),
        name="recurrence_first",
    )(hidden_start, gx_own, ax_other, w_graph, w_input, w_hidden, bias)


def recurrence_later(state, gx_own, gx_other, w_hidden, bias, before, phase, chunk, last):
    snaps, rows, width = gx_other.shape
    hid = w_hidden.shape[0]

    def kernel(state_in, gx_own, gx_other, w_hidden, bias, keep_in, send_in, keep, send, state_out=None):
        core, place = where_am_i()
        at = slice(chunk * rows, (chunk + 1) * rows)
        own = lambda s, columns: gx_own[s, at, columns]
        other = lambda s, columns: gx_other[s, :, columns]

        @pl.when((place == phase) & (core == 0))
        def _():
            run_steps(state_in[...].astype(F32), own, other, keep, send, w_hidden, bias, state_out)

        @pl.when((place == phase) & (core != 0))
        def _():
            run_steps(state_in[...].astype(F32), other, own, send, keep, w_hidden, bias, state_out)

        @pl.when(place != phase)
        def _():
            keep[...] = keep_in[...]
            send[...] = send_in[...]

    part = jax.ShapeDtypeStruct((snaps, rows, hid), BF16)
    return pl.pallas_call(
        kernel,
        out_shape=(part, part) + (() if last else (jax.ShapeDtypeStruct((rows, hid), BF16),)),
        in_specs=[whole()] * 7,
        out_specs=(whole(),) * (2 if last else 3),
        compiler_params=params(),
        cost_estimate=cost(2 * CORES * snaps * rows * hid * 3 * hid * 4, 2**20),
        name="recurrence_later",
    )(state, gx_own, gx_other, w_hidden, bias, *before)


def write_out(out, pieces, nodes):
    snaps, rows, hid = pieces[0][0].shape
    shape = jax.ShapeDtypeStruct((snaps, nodes, hid), BF16)
    count = len(pieces)

    def kernel(*refs):
        sources, target, sems = refs[:count], refs[-2], refs[-1]
        core, _ = where_am_i()
        copies = []
        for i, (_, own, chunk) in enumerate(pieces):
            half = core if own else 1 - core
            start = pl.multiple_of(half * (nodes // CORES) + chunk * rows, rows)
            copies.append(pltpu.make_async_copy(sources[i], target.at[:, pl.ds(start, rows), :], sems.at[i]))
            copies[-1].start()
        for copy in copies:
            copy.wait()

    operands = [array for array, _, _ in pieces] + ([] if out is None else [out])
    return pl.pallas_call(
        kernel,
        out_shape=shape,
        in_specs=[whole()] * count + ([] if out is None else [whole(pl.ANY)]),
        out_specs=whole(pl.ANY),
        scratch_shapes=[pltpu.SemaphoreType.DMA((count,))],
        input_output_aliases={} if out is None else {count: 0},
        compiler_params=params(),
        cost_estimate=cost(0, 2**20),
        name="write_out",
    )(*operands)


def per_device(
    features, tile_values, tile_cols, tile_count, hidden_start, w_graph, w_input, w_hidden, update_bias
):
    snaps, nodes, feats = features.shape
    parts = lax.axis_size("dom")
    sections = lax.axis_size("tm")
    places = sections // CORES
    order = ring_order(parts)
    ahead = [(order[i], order[(i + 1) % parts]) for i in range(parts)]
    back = [(b, a) for a, b in ahead]

    far = parts // 2
    tiles = tile_values
    table = column_table(tile_values, tile_cols, tile_count, order)
    forward = lax.ppermute(features, "dom", ahead)
    reverse = lax.ppermute(features, "dom", back)
    acc = spmm(table, tiles, [features], [0], None)
    dense = dense_tiles(table, tiles, far)
    forward, acc, dense = lax.optimization_barrier((forward, acc, dense))
    waiting = [([forward, reverse], [parts - 1, 1])]
    forward = [forward[s] for s in range(snaps)]
    reverse = [reverse[s] for s in range(snaps)]
    beside = [w_graph, w_input, w_hidden, hidden_start]
    for hop in range(2, far):
        for turn in range(2):
            for s in range(snaps):
                if s % 2 == turn:
                    forward[s] = lax.ppermute(forward[s], "dom", ahead)
                else:
                    reverse[s] = lax.ppermute(reverse[s], "dom", back)
        if hop < far - 1:
            acc = spmm(table, tiles, *waiting.pop(0), acc)
            for s in range(1):
                passing = forward if s % 2 == 0 else reverse
                passing[s], acc = lax.optimization_barrier((passing[s], acc))
        waiting.append((forward + reverse, [parts - hop, hop]))
    arriving = [
        lax.ppermute(forward[s], "dom", ahead) if s % 2 == 0 else lax.ppermute(reverse[s], "dom", back)
        for s in range(snaps)
    ]
    while waiting:
        xs, steps = waiting.pop(0)
        acc = spmm(table, tiles, xs, steps, acc, [] if waiting else beside)
    swap = [(t, t ^ 1) for t in range(sections)]
    keep_ax, send_ax = spmm_last(dense, arriving, acc)
    other_ax = lax.ppermute(send_ax, "tm", swap)
    gx_own = gates(keep_ax, w_graph, w_input)

    bias = update_bias.reshape(1, -1)
    onward = [(t, (t + CORES) % sections) for t in range(sections)]
    hidden, states, gx_other = [], [], []
    for chunk in range(CHUNKS):
        state, keep, send, gx = recurrence_first(
            hidden_start, gx_own, other_ax, w_graph, w_input, w_hidden, bias, chunk
        )
        hidden.append((keep, send))
        states.append(state)
        gx_other.append(gx)
    for phase in range(1, places):
        states = [lax.ppermute(state, "tm", onward) for state in states]
        for chunk in range(CHUNKS):
            last = phase == places - 1
            hidden[chunk] = recurrence_later(
                states[chunk], gx_own, gx_other[chunk], w_hidden, bias, hidden[chunk], phase, chunk, last
            )
            if not last:
                *hidden[chunk], states[chunk] = hidden[chunk]
    pieces = [(keep, True, chunk) for chunk, (keep, _) in enumerate(hidden)]
    pieces += [(lax.ppermute(send, "tm", swap), False, chunk) for chunk, (_, send) in enumerate(hidden)]
    out = write_out(None, pieces[:-1], nodes)
    return write_out(out, pieces[-1:], nodes)


def solution(mesh):
    placed = (
        P("tm", "dom", None),
        P("tm", "dom", None, None, None, None),
        P("tm", "dom", None, None),
        P("tm", "dom", None),
        P("dom", None),
        P(),
        P(),
        P(),
        P(),
    )
    return jax.shard_map(
        per_device, mesh=mesh, in_specs=placed, out_specs=P("tm", "dom", None), check_vma=False
    )
```
